32 devices in a mesh: gx: 4 (over y, core), gy: 8 (over z, x).
Axes of the slice: x: 2, y: 2, z: 4, core: 2. Of those that a mesh axis runs over, the one named last changes fastest.
Arguments:
- right_side: float32 [4096, 64, 128], P(('gx', 'gy')), may hold values from -24 to 24
- fine_coupling: bfloat16 [4096, 64, 4, 64], P(('gx', 'gy')), may hold values from -0.359375 to 0.359375
- fine_diagonal: bfloat16 [4096, 64, 64], P(('gx', 'gy')), may hold values from -0.41 to 6, as said below
- fine_inverse: bfloat16 [4096, 64, 64], P(('gx', 'gy')), may hold values from -1 to 1, as said below
- coarse_coupling: bfloat16 [2048, 64, 8, 64], P(('gx', 'gy')), may hold values from -0.23925781 to 0.23925781
- coarse_diagonal: bfloat16 [2048, 64, 64], P(('gx', 'gy')), may hold values from -0.41 to 6, as said below
- coarse_inverse: bfloat16 [2048, 64, 64], P(('gx', 'gy')), may hold values from -1 to 1, as said below
- coarse_pattern: int32 [2048, 8], P(('gx', 'gy')), may hold values from 0 to 2047, as said below
Outputs:
- fine_iterate: float32 [4096, 64, 128], P(('gx', 'gy'))
- coarse_iterate: float32 [2048, 64, 128], P(('gx', 'gy'))
- next_right_side: float32 [1024, 64, 128], P(('gx', 'gy'))
The draws below stay inside these ranges and needn't reach their ends.
Inputs may be any that keep to these rules, and one draw needn't show every extreme that they name: `coarse_pattern`: the entries of cell c name the eight cells around c on the next level's grid, each once, in an order that differs from cell to cell; an entry whose cell would lie outside the grid names c itself. `fine_diagonal`: each block is a positive diagonal plus smaller off-diagonal entries. `fine_inverse`: each block is the bfloat16 rounding of the inverse of the corresponding diagonal block before its rounding. `coarse_diagonal`: each block is a positive diagonal plus smaller off-diagonal entries. `coarse_inverse`: each block is the bfloat16 rounding of the inverse of the corresponding diagonal block before its rounding.
All inputs are finite; a program needn't handle non-finite values.
Results may differ from the reference program's by a relative error of at most 0.00065.
Values sent between devices are 32-bit elements; how exact they have to be, the bound alone decides.
No kernel may reach another device: no remote copies, remote signals or barrier semaphores. Data moves between devices by JAX's collectives and lax.ppermute only.
A program may use at most 192 MiB of HBM per device.

```python
import math
import jax
import jax.numpy as jnp
from jax import lax

SPECIES = 64
VECTORS = 128
FINE_NEIGHBOURS = 4
COARSE_NEIGHBOURS = 8
BLOCK_X = 4
BLOCK_Y = 32
GRID_X = 16
GRID_Y = 256
FINE_CELLS = 4096
COARSE_CELLS = 2048


def block_pair(key, cell_count, level_tag):
    first_key, second_key = jax.random.split(jax.random.fold_in(key, level_tag))
    leading = jnp.exp(jax.random.uniform(first_key, (cell_count, SPECIES), minval=math.log(3.0), maxval=math.log(6.0)))
    spread_part = jnp.clip(0.12 * jax.random.normal(second_key, (cell_count, SPECIES, SPECIES)), -0.4, 0.4)
    identity = jnp.eye(SPECIES, dtype=jnp.float32)
    blocks = spread_part * (1.0 - identity) + identity * leading[:, :, None]
    inverses = jnp.linalg.inv(blocks)
    return (blocks, inverses)


def draw_fine_diagonal(key, part):
    return block_pair(key, FINE_CELLS, 21)[0].astype(jnp.bfloat16)


def draw_fine_inverse(key, part):
    return block_pair(key, FINE_CELLS, 21)[1].astype(jnp.bfloat16)


def draw_coarse_diagonal(key, part):
    return block_pair(key, COARSE_CELLS, 22)[0].astype(jnp.bfloat16)


def draw_coarse_inverse(key, part):
    return block_pair(key, COARSE_CELLS, 22)[1].astype(jnp.bfloat16)


def draw_coarse_pattern(key, part):
    rows_block = BLOCK_X // 2
    cols_block = BLOCK_Y
    grid_rows = GRID_X // 2
    grid_cols = GRID_Y
    cell_count = grid_rows * grid_cols
    numbers = jnp.arange(cell_count, dtype=jnp.int32)
    per_block = rows_block * cols_block
    blocks_across = grid_cols // cols_block
    owner_block = numbers // per_block
    inside = numbers % per_block
    row_place = owner_block // blocks_across * rows_block + inside // cols_block
    col_place = owner_block % blocks_across * cols_block + inside % cols_block
    row_steps = jnp.array([-1, -1, -1, 0, 0, 1, 1, 1], dtype=jnp.int32)
    col_steps = jnp.array([-1, 0, 1, -1, 1, -1, 0, 1], dtype=jnp.int32)
    row_near = row_place[:, None] + row_steps[None, :]
    col_near = col_place[:, None] + col_steps[None, :]
    inside_grid = (row_near >= 0) & (row_near < grid_rows) & (col_near >= 0) & (col_near < grid_cols)
    target = (row_near // rows_block * blocks_across + col_near // cols_block) * per_block
    target = target + row_near % rows_block * cols_block + col_near % cols_block
    target = jnp.where(inside_grid, target, numbers[:, None])
    scores = jax.random.randint(jax.random.fold_in(key, 12), (cell_count, 8), 0, 1 << 20, dtype=jnp.int32) * 8
    scores = scores + jnp.arange(8, dtype=jnp.int32)[None, :]
    order = jnp.argsort(scores, axis=1)
    picked = jnp.take_along_axis(target, order, axis=1)
    return picked.astype(jnp.int32)


def shard_levels(key, shape, cuts, smallest, top_value):
    factor_of = 1.0
    for dim, blocks in cuts:
        steps = jax.random.uniform(jax.random.fold_in(jax.random.fold_in(key, 6), dim), (blocks,), jnp.float32, smallest / len(cuts), top_value / len(cuts))
        factor_of = factor_of * jnp.repeat(jnp.exp(steps), shape[dim] // blocks).reshape((-1,) + (1,) * (len(shape) - 1 - dim))
    return factor_of


def centred(key, shape, width, limit, cuts=(), held_as=jnp.bfloat16):
    drawn = width * jax.random.normal(key, shape, jnp.float32)
    if cuts:
        drawn = drawn * shard_levels(key, shape, cuts, -0.22, 0.18)
    return jnp.clip(drawn, -limit, limit).astype(held_as)


def setup_inputs(seed: int = 0) -> dict:
    splits = jax.random.split(jax.random.key(seed), 9)
    right_side = centred(splits[0], (FINE_CELLS, SPECIES, VECTORS), 4.0, 24.0, ((0, 32),), jnp.float32)
    fine_coupling = centred(splits[1], (FINE_CELLS, SPECIES, FINE_NEIGHBOURS, SPECIES), 0.06, 0.359375, ((0, 32),))
    fine_diagonal = draw_fine_diagonal(jax.random.fold_in(splits[8], 71), 0)
    fine_inverse = draw_fine_inverse(jax.random.fold_in(splits[8], 71), 0)
    coarse_coupling = centred(splits[4], (COARSE_CELLS, SPECIES, COARSE_NEIGHBOURS, SPECIES), 0.04, 0.23925781, ((0, 32),))
    coarse_diagonal = draw_coarse_diagonal(jax.random.fold_in(splits[8], 71), 0)
    coarse_inverse = draw_coarse_inverse(jax.random.fold_in(splits[8], 71), 0)
    coarse_pattern = draw_coarse_pattern(jax.random.fold_in(splits[8], 71), 0)
    return {"right_side": right_side, "fine_coupling": fine_coupling, "fine_diagonal": fine_diagonal, "fine_inverse": fine_inverse, "coarse_coupling": coarse_coupling, "coarse_diagonal": coarse_diagonal, "coarse_inverse": coarse_inverse, "coarse_pattern": coarse_pattern}


def to_grid(field, rows_block, cols_block, grid_rows, grid_cols):
    species, vectors = (field.shape[1], field.shape[2])
    shaped = field.reshape(grid_rows // rows_block, grid_cols // cols_block, rows_block, cols_block, species, vectors)
    return jnp.transpose(shaped, (0, 2, 1, 3, 4, 5)).reshape(grid_rows, grid_cols, species, vectors)

def per_cell(matrix, vector_b, block_size):
    block_count = vector_b.shape[0] // block_size

    def one_block(number):
        start_cell = number * block_size
        matrix_part = lax.dynamic_slice_in_dim(matrix, start_cell, block_size, 0).astype(jnp.float32)
        vector_part = lax.dynamic_slice_in_dim(vector_b, start_cell, block_size, 0)
        return jnp.einsum('cij,cjv->civ', matrix_part, vector_part, precision=lax.Precision.HIGHEST)
    result = lax.map(one_block, jnp.arange(block_count, dtype=jnp.int32))
    return result.reshape(-1, vector_b.shape[1], vector_b.shape[2])

def operate(vector_b, near_fn, coupling, diagonal, block_size):
    block_count = vector_b.shape[0] // block_size

    def one_block(number):
        start_cell = number * block_size
        near_part = near_fn(number)
        coupling_part = lax.dynamic_slice_in_dim(coupling, start_cell, block_size, 0).astype(jnp.float32)
        diagonal_part = lax.dynamic_slice_in_dim(diagonal, start_cell, block_size, 0).astype(jnp.float32)
        own_part = lax.dynamic_slice_in_dim(vector_b, start_cell, block_size, 0)
        summed = jnp.einsum('cikj,ckjv->civ', coupling_part, near_part, precision=lax.Precision.HIGHEST)
        return summed + jnp.einsum('cij,cjv->civ', diagonal_part, own_part, precision=lax.Precision.HIGHEST)
    result = lax.map(one_block, jnp.arange(block_count, dtype=jnp.int32))
    return result.reshape(-1, vector_b.shape[1], vector_b.shape[2])

def fine_maker(vector_b):
    grid = to_grid(vector_b, BLOCK_X, BLOCK_Y, GRID_X, GRID_Y)
    padded = jnp.pad(grid, ((1, 1), (1, 1), (0, 0), (0, 0)))
    blocks_across = GRID_Y // BLOCK_Y
    species, vectors = (vector_b.shape[1], vector_b.shape[2])

    def near_fn(number):
        row_start = number // blocks_across * BLOCK_X
        col_start = number % blocks_across * BLOCK_Y
        zero = jnp.zeros((), jnp.int32)
        window = lax.dynamic_slice(padded, (row_start, col_start, zero, zero), (BLOCK_X + 2, BLOCK_Y + 2, species, vectors))
        pieces = [window[:-2, 1:-1], window[2:, 1:-1], window[1:-1, :-2], window[1:-1, 2:]]
        return jnp.stack(pieces, axis=2).reshape(BLOCK_X * BLOCK_Y, 4, species, vectors)
    return near_fn

def smooth(side, coupling, diagonal, inverse, maker, block_size):
    first_sweep = per_cell(inverse, side, block_size)
    slack_part = side - operate(first_sweep, maker(first_sweep), coupling, diagonal, block_size)
    second = first_sweep + per_cell(inverse, slack_part, block_size)
    residue = side - operate(second, maker(second), coupling, diagonal, block_size)
    return (second, residue)

def reference(right_side, fine_coupling, fine_diagonal, fine_inverse, coarse_coupling, coarse_diagonal, coarse_inverse, coarse_pattern):
    half_rows = BLOCK_X // 2
    coarse_block = half_rows * BLOCK_Y
    fine_iterate, fine_residue = smooth(right_side, fine_coupling, fine_diagonal, fine_inverse, fine_maker, BLOCK_X * BLOCK_Y)
    coarse_side = fine_residue.reshape(-1, half_rows, 2, BLOCK_Y, SPECIES, VECTORS).sum(axis=2).reshape(-1, SPECIES, VECTORS)
    columns = coarse_pattern.astype(jnp.int32)

    def coarse_maker(vector_b):

        def near_fn(number):
            rows = lax.dynamic_slice_in_dim(columns, number * coarse_block, coarse_block, 0)
            return jnp.take(vector_b, rows, axis=0)
        return near_fn
    coarse_iterate, coarse_residue = smooth(coarse_side, coarse_coupling, coarse_diagonal, coarse_inverse, coarse_maker, coarse_block)
    next_side = coarse_residue.reshape(-1, half_rows, BLOCK_Y // 2, 2, SPECIES, VECTORS).sum(axis=3).reshape(-1, SPECIES, VECTORS)
    return (fine_iterate, coarse_iterate, next_side)
```

```python
import functools

import jax
import jax.numpy as jnp
from jax import lax
from jax.experimental import pallas as pl
from jax.experimental.pallas import tpu as pltpu
from jax.sharding import PartitionSpec as P

BLOCK_X = 4
BLOCK_Y = 32

WIDE = BLOCK_Y + 2
COARSE_X = BLOCK_X // 2
QUARTER = BLOCK_Y // 4
MIDDLE = tuple(range(QUARTER, BLOCK_Y - QUARTER))
ENDS = tuple(q for q in range(BLOCK_Y) if q not in MIDDLE)
UNROLL = 16

F32 = jnp.float32
BF16 = jnp.bfloat16
BOTH = ("gx", "gy")


def split(x):
    high = x.astype(BF16)
    low = (x - high.astype(F32)).astype(BF16)
    return jnp.concatenate([high, low], axis=1)


def fold(x):
    half = x.shape[1] // 2
    return x[:, :half].astype(F32) + x[:, half:].astype(F32)


def dot(*pairs):
    parts = [jnp.dot(a, b, preferred_element_type=F32) for a, b in pairs]
    return fold(functools.reduce(jnp.add, parts))


def row_parity():
    return lax.rem(lax.axis_index("gx"), 2)


def col_parity():
    return lax.rem(lax.axis_index("gy"), 2)


def place(rho, rows):
    parity = row_parity()
    return rho + parity * (rows - 1 - 2 * rho)


def spot(rho, q):
    return (rho + 1) * WIDE + q + 1


def swap_far(rows, cols):
    hop = 2 if cols % 4 == 0 else 1
    pairs = []
    for a in range(rows):
        for b in range(cols):
            partner = a - 1 if a % 2 == 0 else a + 1
            if 0 <= partner < rows:
                pairs.append((a * cols + b, partner * cols + b))
            else:
                pairs.append((a * cols + b, a * cols + (b ^ hop)))
    return pairs


def swap_near(rows, cols):
    return [(a * cols + b, (a ^ 1) * cols + b) for a in range(rows) for b in range(cols)]


def swap_even(rows, cols):
    return [(a * cols + b, a * cols + (b ^ 1)) for a in range(rows) for b in range(cols)]


def swap_odd(rows, cols):
    pairs = []
    for a in range(rows):
        for b in range(cols):
            partner = b - 1 if b % 2 == 0 else b + 1
            if 0 <= partner < cols:
                pairs.append((a * cols + b, a * cols + partner))
            else:
                pairs.append((a * cols + b, (a ^ 1) * cols + b))
    return pairs


def far_is_inside():
    gx = lax.axis_index("gx")
    return jnp.where(row_parity() == 0, gx > 0, gx < lax.axis_size("gx") - 1)


def odd_is_inside():
    gy = lax.axis_index("gy")
    return jnp.where(col_parity() == 0, gy > 0, gy < lax.axis_size("gy") - 1)


def write_sides(grid, even_halo, odd_halo, rows):
    parity = col_parity()
    even_col = jnp.where(parity == 0, BLOCK_Y, -1)
    odd_col = BLOCK_Y - 1 - even_col
    inside = odd_is_inside()
    for rho in range(rows):
        grid[spot(rho, even_col)] = split(even_halo[rho])
        grid[spot(rho, odd_col)] = split(jnp.where(inside, odd_halo[rho], 0.0))


def read_sides(grid, even_send, odd_send, rows):
    parity = col_parity()
    even_col = jnp.where(parity == 0, BLOCK_Y - 1, 0)
    odd_col = BLOCK_Y - 1 - even_col
    for rho in range(rows):
        even_send[rho] = fold(grid[spot(rho, even_col)])
        odd_send[rho] = fold(grid[spot(rho, odd_col)])


def write_row(grid, halo, rho, cols, inside=None):
    for n, q in enumerate(cols):
        value = halo[n]
        if inside is not None:
            value = jnp.where(inside, value, 0.0)
        grid[spot(rho, q)] = split(value)


def read_row(grid, send, rho, cols):
    for n, q in enumerate(cols):
        send[n] = fold(grid[spot(rho, q)])


def over_rows(first, last, body):
    parts = BLOCK_Y // UNROLL

    def step(n, carry):
        body(first + n // parts, lax.rem(n, parts) * UNROLL)
        return carry

    lax.fori_loop(0, (last - first) * parts, step, 0)


def send_out(scratch, n, out, first, count, sem):
    copy = pltpu.make_async_copy(scratch.at[pl.ds(n, count)], out.at[pl.ds(first, count)], sem)
    copy.start()
    return copy


def stretches(cols):
    found = []
    for n, q in enumerate(cols):
        if found and found[-1][1] + found[-1][2] == q:
            found[-1][2] += 1
        else:
            found.append([n, q, 1])
    return found


def with_zeros(own, after):
    none = jnp.zeros(own.shape, BF16)
    return jnp.concatenate([own, none] if after else [none, own], axis=0)


def smoothed(blocks, cell, side):
    species = side.shape[0]
    return dot((blocks[cell, :, -2 * species :], with_zeros(split(side), False)))


def fine_cell(rho, q):
    return place(rho, BLOCK_X) * BLOCK_Y + q


def fine_apply(rho, q, blocks, grid):
    cell = fine_cell(rho, q)
    species = blocks.shape[1]
    here = spot(rho, q)
    step = WIDE * (1 - 2 * row_parity())
    near = jnp.concatenate([grid[here - step], grid[here + step], grid[here - 1], grid[here + 1]], axis=0)
    return dot(
        (blocks[cell, :, : 4 * species], near), (blocks[cell, :, 4 * species :], with_zeros(grid[here], True))
    )


def fine_second(rho, cols, blocks, grid, side, change, iterate, n, far=None):
    for q in cols:
        cell = fine_cell(rho, q)
        side[cell] = side[cell] - fine_apply(rho, q, blocks, grid)
    for m, q in enumerate(cols):
        cell = fine_cell(rho, q)
        here = spot(rho, q)
        step = smoothed(blocks, cell, side[cell])
        change[here] = split(step)
        iterate[n + m] = fold(grid[here]) + step
        if far is not None:
            far[m] = step


def fine_left(rho, q, blocks, side, change):
    return side[fine_cell(rho, q)] - fine_apply(rho, q, blocks, change)


def start_kernel(right, inverse, blocks, grid, side, far_m, far_n, inverse_here, sems):
    species = inverse.shape[0]
    part = species // 2
    loads = [
        pltpu.make_async_copy(inverse.at[pl.ds(n * part, part)], inverse_here.at[pl.ds(n * part, part)], sems.at[n])
        for n in range(2)
    ]
    for rho in range(BLOCK_X):
        row = pl.ds(fine_cell(rho, 0), BLOCK_Y)
        loads.append(pltpu.make_async_copy(right.at[row], side.at[row], sems.at[2 + rho]))
    for load in loads:
        load.start()
    for n in range(2):
        loads[n].wait()
        some = inverse_here[n * part : (n + 1) * part]
        both = jnp.concatenate([jnp.zeros(some.shape, BF16), some], axis=1)
        blocks[:, n * part : (n + 1) * part, 4 * species :] = jnp.transpose(both, (2, 0, 1))
    loads[2].wait()
    for cols, send in ((MIDDLE, far_m), (ENDS, far_n)):
        for n, q in enumerate(cols):
            cell = fine_cell(0, q)
            first = smoothed(blocks, cell, side[cell])
            grid[spot(0, q)] = split(first)
            send[n] = first
    for load in loads[3:]:
        load.wait()


def first_kernel(side, blocks, grid_in, grid, near, even, odd):
    def body(rho, start):
        for q in range(UNROLL):
            cell = fine_cell(rho, start + q)
            grid[spot(rho, start + q)] = split(smoothed(blocks, cell, side[cell]))

    over_rows(1, BLOCK_X, body)
    read_row(grid, near, BLOCK_X - 1, range(BLOCK_Y))
    read_sides(grid, even, odd, BLOCK_X)


def fine_blocks_kernel(coupling, diagonal, inverse, blocks_in, blocks):
    species = coupling.shape[0]
    part = species // 2
    for first in range(0, species, part):
        rows = slice(first, first + part)
        blocks[:, rows, : 4 * species] = jnp.transpose(coupling[rows], (2, 0, 1))
        both = jnp.concatenate([diagonal[rows], inverse[rows]], axis=1)
        blocks[:, rows, 4 * species :] = jnp.transpose(both, (2, 0, 1))


def fine_inner_kernel(blocks, near_h, even_h, odd_h, grid_in, side_in, grid, side, change, out, near, iterate, sems):
    write_row(grid, near_h, BLOCK_X, range(BLOCK_Y))
    write_sides(grid, even_h, odd_h, BLOCK_X)

    def body(rho, start):
        n = (rho - 1) * BLOCK_Y + start
        fine_second(rho, [start + q for q in range(UNROLL)], blocks, grid, side, change, iterate, n)
        send_out(iterate, n, out, fine_cell(rho, start), UNROLL, sems.at[n // UNROLL])

    over_rows(1, BLOCK_X, body)
    read_row(change, near, BLOCK_X - 1, range(BLOCK_Y))
    for n in range((BLOCK_X - 1) * BLOCK_Y // UNROLL):
        part = iterate.at[pl.ds(n * UNROLL, UNROLL)]
        pltpu.make_async_copy(part, out.at[pl.ds(0, UNROLL)], sems.at[n]).wait()


def fine_outer_kernel(
    cols, sides, blocks, far_h, grid_in, side_in, change_in, out_in, grid, side, change, out, far, *rest
):
    *sends, iterate, sems = rest
    write_row(grid, far_h, -1, cols, far_is_inside())
    fine_second(0, cols, blocks, grid, side, change, iterate, 0, far)
    copies = [
        send_out(iterate, n, out, fine_cell(0, q), count, sems.at[k])
        for k, (n, q, count) in enumerate(stretches(cols))
    ]
    if sides:
        read_sides(change, *sends, BLOCK_X)
    for copy in copies:
        copy.wait()


def next_first(rho, cols, side, blocks, grid, far=None):
    for n, q in enumerate(cols):
        cell = place(rho, COARSE_X) * BLOCK_Y + q
        first = smoothed(blocks, cell, side[rho * BLOCK_Y + q])
        grid[spot(rho, q)] = split(first)
        if far is not None:
            far[n] = first


def left_inner_kernel(blocks, side, coarse_blocks, near_h, even_h, odd_h, change_in, change, coarse_side, coarse_grid):
    write_row(change, near_h, BLOCK_X, range(BLOCK_Y))
    write_sides(change, even_h, odd_h, BLOCK_X)

    def pairs(rho, start):
        for q in range(UNROLL):
            upper = fine_left(2 * rho, start + q, blocks, side, change)
            lower = fine_left(2 * rho + 1, start + q, blocks, side, change)
            coarse_side[rho * BLOCK_Y + start + q] = upper + lower
        next_first(rho, [start + q for q in range(UNROLL)], coarse_side, coarse_blocks, coarse_grid)

    over_rows(1, COARSE_X, pairs)

    def single(rho, start):
        for q in range(UNROLL):
            coarse_side[start + q] = fine_left(rho, start + q, blocks, side, change)

    over_rows(1, 2, single)


def left_outer_kernel(
    cols, sides, blocks, side, coarse_blocks, far_h, change_in, coarse_in, grid_in, change, coarse_side, coarse_grid, *sends
):
    write_row(change, far_h, -1, cols, far_is_inside())
    for q in cols:
        coarse_side[q] = coarse_side[q] + fine_left(0, q, blocks, side, change)
    next_first(0, cols, coarse_side, coarse_blocks, coarse_grid, None if sides else sends[0])
    if sides:
        read_sides(coarse_grid, *sends, COARSE_X)


def coarse_blocks_kernel(coupling, diagonal, inverse, after, blocks):
    species = coupling.shape[1]
    first = pl.program_id(0) * coupling.shape[0]
    for n in range(coupling.shape[0]):
        blocks[first + n, :, : 8 * species] = coupling[n].reshape(species, 8 * species)
        blocks[first + n, :, 8 * species :] = jnp.concatenate([diagonal[n], inverse[n]], axis=1)


def coarse_apply(rho, q, places, blocks, grid):
    cell = place(rho, COARSE_X) * BLOCK_Y + q
    species = blocks.shape[1]
    near = jnp.concatenate([grid[places[k, cell]] for k in range(8)], axis=0)
    return dot(
        (blocks[cell, :, : 8 * species], near), (blocks[cell, :, 8 * species :], with_zeros(grid[spot(rho, q)], True))
    )


def coarse_second(rho, cols, places, blocks, grid, side, change, iterate, n, far=None):
    for q in cols:
        here = rho * BLOCK_Y + q
        side[here] = side[here] - coarse_apply(rho, q, places, blocks, grid)
    for m, q in enumerate(cols):
        here = spot(rho, q)
        step = smoothed(blocks, place(rho, COARSE_X) * BLOCK_Y + q, side[rho * BLOCK_Y + q])
        change[here] = split(step)
        iterate[n + m] = fold(grid[here]) + step
        if far is not None:
            far[m] = step


def pack_kernel(cols, even_h, odd_h, grid_in, grid, far, near):
    write_sides(grid, even_h, odd_h, COARSE_X)
    read_row(grid, far, 0, cols + (-1, BLOCK_Y))
    read_row(grid, near, COARSE_X - 1, range(-1, BLOCK_Y + 1))


def coarse_inner_kernel(places, blocks, near_h, grid_in, side_in, grid, side, change, out, iterate, sems):
    write_row(grid, near_h, COARSE_X, range(-1, BLOCK_Y + 1))

    def body(rho, start):
        n = (rho - 1) * BLOCK_Y + start
        cell = place(rho, COARSE_X) * BLOCK_Y + start
        coarse_second(rho, [start + q for q in range(UNROLL)], places, blocks, grid, side, change, iterate, n)
        send_out(iterate, n, out, cell, UNROLL, sems.at[n // UNROLL])

    over_rows(1, COARSE_X, body)
    for n in range((COARSE_X - 1) * BLOCK_Y // UNROLL):
        part = iterate.at[pl.ds(n * UNROLL, UNROLL)]
        pltpu.make_async_copy(part, out.at[pl.ds(0, UNROLL)], sems.at[n]).wait()


def coarse_outer_kernel(
    came, cols, sides, places, blocks, far_h, grid_in, side_in, change_in, out_in, grid, side, change, out, *rest
):
    *sends, iterate, sems = rest
    write_row(grid, far_h, -1, came)
    coarse_second(0, cols, places, blocks, grid, side, change, iterate, 0, None if sides else sends[0])
    copies = [
        send_out(iterate, n, out, place(0, COARSE_X) * BLOCK_Y + q, count, sems.at[k])
        for k, (n, q, count) in enumerate(stretches(cols))
    ]
    if sides:
        read_sides(change, *sends, COARSE_X)
    for copy in copies:
        copy.wait()


def coarse_left(rho, q, places, blocks, side, change):
    return side[rho * BLOCK_Y + q] - coarse_apply(rho, q, places, blocks, change)


def last_pair(rho, q, places, blocks, side, change):
    return coarse_left(rho, q, places, blocks, side, change) + coarse_left(rho, q + 1, places, blocks, side, change)


def last_inner_kernel(places, blocks, side, near_h, change_in, change, out, below, sems):
    write_row(change, near_h, COARSE_X, range(-1, BLOCK_Y + 1))
    count = UNROLL // 2

    def body(rho, start):
        n = ((rho - 1) * BLOCK_Y + start) // 2
        for q in range(count):
            below[n + q] = last_pair(rho, start + 2 * q, places, blocks, side, change)
        send_out(below, n, out, (place(rho, COARSE_X) * BLOCK_Y + start) // 2, count, sems.at[n // count])

    over_rows(1, COARSE_X, body)
    for n in range((COARSE_X - 1) * BLOCK_Y // UNROLL):
        part = below.at[pl.ds(n * count, count)]
        pltpu.make_async_copy(part, out.at[pl.ds(0, count)], sems.at[n]).wait()


def last_outer_kernel(came, cols, places, blocks, side, far_h, change_in, out_in, change, out, below, sems):
    write_row(change, far_h, -1, came)
    pairs = [q // 2 for q in cols[::2]]
    for n, q in enumerate(pairs):
        below[n] = last_pair(0, 2 * q, places, blocks, side, change)
    copies = [
        send_out(below, n, out, place(0, COARSE_X) * BLOCK_Y // 2 + q, count, sems.at[k])
        for k, (n, q, count) in enumerate(stretches(pairs))
    ]
    for copy in copies:
        copy.wait()


IN_VMEM = pl.BlockSpec(memory_space=pltpu.VMEM)
IN_SMEM = pl.BlockSpec(memory_space=pltpu.SMEM)
IN_HBM = pl.BlockSpec(memory_space=pltpu.HBM)


def run(name, kernel, outs, args, aliases=(), scalars=(), far_args=(), far_outs=(), scratch=(), after=()):
    count = len(args)
    args = list(args) + list(after)
    specs = [IN_SMEM if n in scalars else IN_HBM if n in far_args else IN_VMEM for n in range(len(args))]
    args = [
        x if n in scalars or n in far_args else pltpu.with_memory_space_constraint(x, pltpu.VMEM)
        for n, x in enumerate(args)
    ]

    def body(*refs):
        kernel(*refs[:count], *refs[len(args) :])

    called = pl.pallas_call(
        body,
        out_shape=tuple(
            (pltpu.HBM if n in far_outs else pltpu.VMEM)(shape, dtype) for n, (shape, dtype) in enumerate(outs)
        ),
        in_specs=specs,
        out_specs=tuple(IN_HBM if n in far_outs else IN_VMEM for n in range(len(outs))),
        scratch_shapes=list(scratch),
        input_output_aliases=dict(aliases),
        compiler_params=pltpu.CompilerParams(vmem_limit_bytes=8 * 2**20),
        cost_estimate=pl.CostEstimate(flops=1, bytes_accessed=1, transcendentals=0),
        name=name,
    )
    return called(*args)


def coarse_blocks_call(coupling, diagonal, inverse, after):
    cells, species = coupling.shape[:2]
    part = cells // 8
    return pl.pallas_call(
        coarse_blocks_kernel,
        grid=(cells // part,),
        out_shape=pltpu.VMEM((cells, species, 10 * species), BF16),
        in_specs=[
            pl.BlockSpec((part,) + coupling.shape[1:], lambda n: (n, 0, 0, 0)),
            pl.BlockSpec((part,) + diagonal.shape[1:], lambda n: (n, 0, 0)),
            pl.BlockSpec((part,) + inverse.shape[1:], lambda n: (n, 0, 0)),
            IN_VMEM,
        ],
        out_specs=IN_VMEM,
        compiler_params=pltpu.CompilerParams(vmem_limit_bytes=8 * 2**20),
        cost_estimate=pl.CostEstimate(flops=1, bytes_accessed=1, transcendentals=0),
        name="coarse_blocks",
    )(coupling, diagonal, inverse, pltpu.with_memory_space_constraint(after, pltpu.VMEM))


def coarse_places(pattern):
    blocks_across = lax.axis_size("gy")
    pattern = pattern.T
    per_block = COARSE_X * BLOCK_Y
    owner = pattern // per_block
    inside = pattern % per_block
    row = owner // blocks_across * COARSE_X + inside // BLOCK_Y - lax.axis_index("gx") * COARSE_X
    col = owner % blocks_across * BLOCK_Y + inside % BLOCK_Y - lax.axis_index("gy") * BLOCK_Y
    rho = jnp.where(row_parity() == 0, row, COARSE_X - 1 - row)
    return (rho + 1) * WIDE + col + 1


def on_device(
    right_side,
    fine_coupling,
    fine_diagonal,
    fine_inverse,
    coarse_coupling,
    coarse_diagonal,
    coarse_inverse,
    coarse_pattern,
):
    cells, species, vectors = right_side.shape
    coarse_cells = coarse_coupling.shape[0]
    rows, cols = lax.axis_size("gx"), lax.axis_size("gy")
    far_pairs, near_pairs = swap_far(rows, cols), swap_near(rows, cols)
    even_pairs, odd_pairs = swap_even(rows, cols), swap_odd(rows, cols)

    def far(x):
        return lax.ppermute(x, BOTH, far_pairs)

    def near(x):
        return lax.ppermute(x, BOTH, near_pairs)

    def even(x):
        return lax.ppermute(x, BOTH, even_pairs)

    def odd(x):
        return lax.ppermute(x, BOTH, odd_pairs)

    def field(count):
        return ((count, species, vectors), F32)

    def row_scratch(count):
        return [pltpu.VMEM((count, species, vectors), F32), pltpu.SemaphoreType.DMA((max(2, count // 8),))]

    def padded(count):
        return (((count + 2) * WIDE, species, 2 * vectors), BF16)

    fine_blocks = ((cells, species, 6 * species), BF16)
    coupling = jnp.transpose(fine_coupling, (1, 2, 3, 0)).reshape(species, 4 * species, cells)
    diagonal = jnp.transpose(fine_diagonal, (1, 2, 0))
    inverse = jnp.transpose(fine_inverse, (1, 2, 0))
    places = coarse_places(coarse_pattern)
    middle, ends = len(MIDDLE), len(ENDS)

    blocks, grid, side, far_m, far_n = run(
        "start",
        start_kernel,
        [fine_blocks, padded(BLOCK_X), field(cells), field(middle), field(ends)],
        [right_side, inverse],
        far_args=(0, 1),
        scratch=[pltpu.VMEM(inverse.shape, BF16), pltpu.SemaphoreType.DMA((2 + BLOCK_X,))],
    )
    far_m, far_n = far(far_m), far(far_n)
    grid, near_s, even_s, odd_s = run(
        "first",
        first_kernel,
        [padded(BLOCK_X), field(BLOCK_Y), field(BLOCK_X), field(BLOCK_X)],
        [side, blocks, grid],
        [(2, 0)],
    )
    near_h, even_h, odd_h = near(near_s), even(even_s), odd(odd_s)
    (blocks,) = run(
        "fine_blocks",
        fine_blocks_kernel,
        [fine_blocks],
        [coupling, diagonal, inverse, blocks],
        [(3, 0)],
        after=[near_s],
    )
    grid, side, change, iterate, near_s = run(
        "fine_inner",
        fine_inner_kernel,
        [padded(BLOCK_X), field(cells), padded(BLOCK_X), field(cells), field(BLOCK_Y)],
        [blocks, near_h, even_h, odd_h, grid, side],
        [(4, 0), (5, 1)],
        far_outs=(3,),
        scratch=row_scratch((BLOCK_X - 1) * BLOCK_Y),
    )
    near_h = near(near_s)
    coarse_blocks = coarse_blocks_call(coarse_coupling, coarse_diagonal, coarse_inverse, near_s)
    state = [padded(BLOCK_X), field(cells), padded(BLOCK_X), field(cells)]
    same = [(2, 0), (3, 1), (4, 2), (5, 3)]
    grid, side, change, iterate, far_m = run(
        "fine_middle",
        functools.partial(fine_outer_kernel, MIDDLE, False),
        state + [field(middle)],
        [blocks, far_m, grid, side, change, iterate],
        same,
        far_args=(5,),
        far_outs=(3,),
        scratch=row_scratch(middle),
        after=[coarse_blocks],
    )
    far_m = far(far_m)
    grid, side, change, fine_iterate, far_n, even_s, odd_s = run(
        "fine_ends",
        functools.partial(fine_outer_kernel, ENDS, True),
        state + [field(ends), field(BLOCK_X), field(BLOCK_X)],
        [blocks, far_n, grid, side, change, iterate],
        same,
        far_args=(5,),
        far_outs=(3,),
        scratch=row_scratch(ends),
    )
    far_n = far(far_n)
    even_h, odd_h = even(even_s), odd(odd_s)

    state = [padded(BLOCK_X), field(coarse_cells), padded(COARSE_X)]
    change, coarse_side, coarse_grid = run(
        "left_inner",
        left_inner_kernel,
        state,
        [blocks, side, coarse_blocks, near_h, even_h, odd_h, change],
        [(6, 0)],
    )
    same = [(4, 0), (5, 1), (6, 2)]
    change, coarse_side, coarse_grid, far_m = run(
        "left_middle",
        functools.partial(left_outer_kernel, MIDDLE, False),
        state + [field(middle)],
        [blocks, side, coarse_blocks, far_m, change, coarse_side, coarse_grid],
        same,
    )
    far_m = far(far_m)
    change, coarse_side, coarse_grid, even_s, odd_s = run(
        "left_ends",
        functools.partial(left_outer_kernel, ENDS, True),
        state + [field(COARSE_X), field(COARSE_X)],
        [blocks, side, coarse_blocks, far_n, change, coarse_side, coarse_grid],
        same,
    )
    even_h, odd_h = even(even_s), odd(odd_s)
    coarse_grid, far_n, near_s = run(
        "pack_first",
        functools.partial(pack_kernel, ENDS),
        [padded(COARSE_X), field(ends + 2), field(BLOCK_Y + 2)],
        [even_h, odd_h, coarse_grid],
        [(2, 0)],
    )
    far_n, near_h = far(far_n), near(near_s)

    state = [padded(COARSE_X), field(coarse_cells), padded(COARSE_X), field(coarse_cells)]
    coarse_grid, coarse_side, coarse_change, iterate = run(
        "coarse_inner",
        coarse_inner_kernel,
        state,
        [places, coarse_blocks, near_h, coarse_grid, coarse_side],
        [(3, 0), (4, 1)],
        scalars=(0,),
        far_outs=(3,),
        scratch=row_scratch((COARSE_X - 1) * BLOCK_Y),
    )
    inner = MIDDLE[1:-1]
    outer = tuple(q for q in range(BLOCK_Y) if q not in inner)
    same = [(3, 0), (4, 1), (5, 2), (6, 3)]
    coarse_grid, coarse_side, coarse_change, iterate, far_m = run(
        "coarse_middle",
        functools.partial(coarse_outer_kernel, MIDDLE, inner, False),
        state + [field(len(inner))],
        [places, coarse_blocks, far_m, coarse_grid, coarse_side, coarse_change, iterate],
        same,
        scalars=(0,),
        far_args=(6,),
        far_outs=(3,),
        scratch=row_scratch(len(inner)),
    )
    far_m = far(far_m)
    coarse_grid, coarse_side, coarse_change, coarse_iterate, even_s, odd_s = run(
        "coarse_ends",
        functools.partial(coarse_outer_kernel, ENDS + (-1, BLOCK_Y), outer, True),
        state + [field(COARSE_X), field(COARSE_X)],
        [places, coarse_blocks, far_n, coarse_grid, coarse_side, coarse_change, iterate],
        same,
        scalars=(0,),
        far_args=(6,),
        far_outs=(3,),
        scratch=row_scratch(len(outer)),
    )
    even_h, odd_h = even(even_s), odd(odd_s)
    coarse_change, far_n, near_s = run(
        "pack_second",
        functools.partial(pack_kernel, outer),
        [padded(COARSE_X), field(len(outer) + 2), field(BLOCK_Y + 2)],
        [even_h, odd_h, coarse_change],
        [(2, 0)],
    )
    far_n, near_h = far(far_n), near(near_s)

    state = [padded(COARSE_X), field(coarse_cells // 2)]
    coarse_change, next_side = run(
        "last_inner",
        last_inner_kernel,
        state,
        [places, coarse_blocks, coarse_side, near_h, coarse_change],
        [(4, 0)],
        scalars=(0,),
        far_outs=(1,),
        scratch=row_scratch((COARSE_X - 1) * BLOCK_Y // 2),
    )
    core = inner[1:-1]
    rest = tuple(q for q in range(BLOCK_Y) if q not in core)
    coarse_change, next_side = run(
        "last_middle",
        functools.partial(last_outer_kernel, inner, core),
        state,
        [places, coarse_blocks, coarse_side, far_m, coarse_change, next_side],
        [(4, 0), (5, 1)],
        scalars=(0,),
        far_args=(5,),
        far_outs=(1,),
        scratch=row_scratch(len(core) // 2),
    )
    coarse_change, next_side = run(
        "last_ends",
        functools.partial(last_outer_kernel, outer + (-1, BLOCK_Y), rest),
        state,
        [places, coarse_blocks, coarse_side, far_n, coarse_change, next_side],
        [(4, 0), (5, 1)],
        scalars=(0,),
        far_args=(5,),
        far_outs=(1,),
        scratch=row_scratch(len(rest) // 2),
    )
    return (fine_iterate, coarse_iterate, next_side)


def solution(mesh):
    placed = (
        P(BOTH, None, None),
        P(BOTH, None, None, None),
        P(BOTH, None, None),
        P(BOTH, None, None),
        P(BOTH, None, None, None),
        P(BOTH, None, None),
        P(BOTH, None, None),
        P(BOTH, None),
    )
    return jax.shard_map(
        on_device,
        mesh=mesh,
        in_specs=placed,
        out_specs=(P(BOTH, None, None), P(BOTH, None, None), P(BOTH, None, None)),
        check_vma=False,
    )
```

```python
import functools

import jax
import jax.numpy as jnp
from jax import lax
from jax.experimental import pallas as pl
from jax.experimental.pallas import tpu as pltpu
from jax.sharding import PartitionSpec as P

BLOCK_X = 4
BLOCK_Y = 32

WIDE = BLOCK_Y + 2
COARSE_X = BLOCK_X // 2
QUARTER = BLOCK_Y // 4
MIDDLE = tuple(range(QUARTER, BLOCK_Y - QUARTER))
ENDS = tuple(q for q in range(BLOCK_Y) if q not in MIDDLE)
UNROLL = 16

F32 = jnp.float32
BF16 = jnp.bfloat16
BOTH = ("gx", "gy")


def split(x):
    high = x.astype(BF16)
    low = (x - high.astype(F32)).astype(BF16)
    return jnp.concatenate([high, low], axis=1)


def fold(x):
    half = x.shape[1] // 2
    return x[:, :half].astype(F32) + x[:, half:].astype(F32)


def dot(*pairs):
    parts = [jnp.dot(a, b, preferred_element_type=F32) for a, b in pairs]
    return fold(functools.reduce(jnp.add, parts))


def row_parity():
    return lax.rem(lax.axis_index("gx"), 2)


def col_parity():
    return lax.rem(lax.axis_index("gy"), 2)


def place(rho, rows):
    parity = row_parity()
    return rho + parity * (rows - 1 - 2 * rho)


def spot(rho, q):
    return (rho + 1) * WIDE + q + 1


def swap_far(rows, cols):
    hop = 2 if cols % 4 == 0 else 1
    pairs = []
    for a in range(rows):
        for b in range(cols):
            partner = a - 1 if a % 2 == 0 else a + 1
            if 0 <= partner < rows:
                pairs.append((a * cols + b, partner * cols + b))
            else:
                pairs.append((a * cols + b, a * cols + (b ^ hop)))
    return pairs


def swap_near(rows, cols):
    return [(a * cols + b, (a ^ 1) * cols + b) for a in range(rows) for b in range(cols)]


def swap_even(rows, cols):
    return [(a * cols + b, a * cols + (b ^ 1)) for a in range(rows) for b in range(cols)]


def swap_odd(rows, cols):
    pairs = []
    for a in range(rows):
        for b in range(cols):
            partner = b - 1 if b % 2 == 0 else b + 1
            if 0 <= partner < cols:
                pairs.append((a * cols + b, a * cols + partner))
            else:
                pairs.append((a * cols + b, (a ^ 1) * cols + b))
    return pairs


def far_is_inside():
    gx = lax.axis_index("gx")
    return jnp.where(row_parity() == 0, gx > 0, gx < lax.axis_size("gx") - 1)


def odd_is_inside():
    gy = lax.axis_index("gy")
    return jnp.where(col_parity() == 0, gy > 0, gy < lax.axis_size("gy") - 1)


def write_sides(grid, even_halo, odd_halo, rows):
    parity = col_parity()
    even_col = jnp.where(parity == 0, BLOCK_Y, -1)
    odd_col = BLOCK_Y - 1 - even_col
    inside = odd_is_inside()
    for rho in range(rows):
        grid[spot(rho, even_col)] = split(even_halo[rho])
        grid[spot(rho, odd_col)] = split(jnp.where(inside, odd_halo[rho], 0.0))


def read_sides(grid, even_send, odd_send, rows):
    parity = col_parity()
    even_col = jnp.where(parity == 0, BLOCK_Y - 1, 0)
    odd_col = BLOCK_Y - 1 - even_col
    for rho in range(rows):
        even_send[rho] = fold(grid[spot(rho, even_col)])
        odd_send[rho] = fold(grid[spot(rho, odd_col)])


def write_row(grid, halo, rho, cols, inside=None):
    for n, q in enumerate(cols):
        value = halo[n]
        if inside is not None:
            value = jnp.where(inside, value, 0.0)
        grid[spot(rho, q)] = split(value)


def read_row(grid, send, rho, cols):
    for n, q in enumerate(cols):
        send[n] = fold(grid[spot(rho, q)])


def over_rows(first, last, body):
    parts = BLOCK_Y // UNROLL

    def step(n, carry):
        body(first + n // parts, lax.rem(n, parts) * UNROLL)
        return carry

    lax.fori_loop(0, (last - first) * parts, step, 0)


def send_out(scratch, n, out, first, count, sem):
    copy = pltpu.make_async_copy(scratch.at[pl.ds(n, count)], out.at[pl.ds(first, count)], sem)
    copy.start()
    return copy


def stretches(cols):
    found = []
    for n, q in enumerate(cols):
        if found and found[-1][1] + found[-1][2] == q:
            found[-1][2] += 1
        else:
            found.append([n, q, 1])
    return found


def with_zeros(own, after):
    none = jnp.zeros(own.shape, BF16)
    return jnp.concatenate([own, none] if after else [none, own], axis=0)


def smoothed(blocks, cell, side):
    species = side.shape[0]
    return dot((blocks[cell, :, -2 * species :], with_zeros(split(side), False)))


def fine_cell(rho, q):
    return place(rho, BLOCK_X) * BLOCK_Y + q


def fine_apply(rho, q, blocks, grid):
    cell = fine_cell(rho, q)
    species = blocks.shape[1]
    here = spot(rho, q)
    step = WIDE * (1 - 2 * row_parity())
    near = jnp.concatenate([grid[here - step], grid[here + step], grid[here - 1], grid[here + 1]], axis=0)
    return dot(
        (blocks[cell, :, : 4 * species], near), (blocks[cell, :, 4 * species :], with_zeros(grid[here], True))
    )


def fine_second(rho, cols, blocks, grid, side, change, iterate, n, far=None):
    for q in cols:
        cell = fine_cell(rho, q)
        side[cell] = side[cell] - fine_apply(rho, q, blocks, grid)
    for m, q in enumerate(cols):
        cell = fine_cell(rho, q)
        here = spot(rho, q)
        step = smoothed(blocks, cell, side[cell])
        change[here] = split(step)
        iterate[n + m] = fold(grid[here]) + step
        if far is not None:
            far[m] = step


def fine_left(rho, q, blocks, side, change):
    return side[fine_cell(rho, q)] - fine_apply(rho, q, blocks, change)


def start_kernel(right, inverse, blocks, grid, side, far_m, far_n, inverse_here, sems):
    species = inverse.shape[0]
    part = species // 2
    loads = [
        pltpu.make_async_copy(inverse.at[pl.ds(n * part, part)], inverse_here.at[pl.ds(n * part, part)], sems.at[n])
        for n in range(2)
    ]
    for rho in range(BLOCK_X):
        row = pl.ds(fine_cell(rho, 0), BLOCK_Y)
        loads.append(pltpu.make_async_copy(right.at[row], side.at[row], sems.at[2 + rho]))
    for load in loads:
        load.start()
    for n in range(2):
        loads[n].wait()
        some = inverse_here[n * part : (n + 1) * part]
        both = jnp.concatenate([jnp.zeros(some.shape, BF16), some], axis=1)
        blocks[:, n * part : (n + 1) * part, 4 * species :] = jnp.transpose(both, (2, 0, 1))
    loads[2].wait()
    for cols, send in ((MIDDLE, far_m), (ENDS, far_n)):
        for n, q in enumerate(cols):
            cell = fine_cell(0, q)
            first = smoothed(blocks, cell, side[cell])
            grid[spot(0, q)] = split(first)
            send[n] = first
    for load in loads[3:]:
        load.wait()


def first_kernel(side, blocks, grid_in, grid, near, even, odd):
    def body(rho, start):
        for q in range(UNROLL):
            cell = fine_cell(rho, start + q)
            grid[spot(rho, start + q)] = split(smoothed(blocks, cell, side[cell]))

    over_rows(1, BLOCK_X, body)
    read_row(grid, near, BLOCK_X - 1, range(BLOCK_Y))
    read_sides(grid, even, odd, BLOCK_X)


def fine_blocks_kernel(coupling, diagonal, inverse, blocks_in, blocks):
    species = coupling.shape[0]
    part = species // 2
    for first in range(0, species, part):
        rows = slice(first, first + part)
        blocks[:, rows, : 4 * species] = jnp.transpose(coupling[rows], (2, 0, 1))
        both = jnp.concatenate([diagonal[rows], inverse[rows]], axis=1)
        blocks[:, rows, 4 * species :] = jnp.transpose(both, (2, 0, 1))


def fine_inner_kernel(
    blocks, near_h, even_h, odd_h, grid_in, side_in, change_in, out_in, grid, side, change, out, near, iterate, sems
):
    write_row(grid, near_h, BLOCK_X, range(BLOCK_Y))
    write_sides(grid, even_h, odd_h, BLOCK_X)

    def body(rho, start):
        n = (rho - 1) * BLOCK_Y + start
        fine_second(rho, [start + q for q in range(UNROLL)], blocks, grid, side, change, iterate, n)
        send_out(iterate, n, out, fine_cell(rho, start), UNROLL, sems.at[n // UNROLL])

    over_rows(1, BLOCK_X, body)
    read_row(change, near, BLOCK_X - 1, range(BLOCK_Y))
    for n in range((BLOCK_X - 1) * BLOCK_Y // UNROLL):
        part = iterate.at[pl.ds(n * UNROLL, UNROLL)]
        pltpu.make_async_copy(part, out.at[pl.ds(0, UNROLL)], sems.at[n]).wait()


def fine_middle_kernel(cols, blocks, far_h, grid_in, side_in, *rest):
    fine_outer(cols, False, blocks, far_h, *rest)


def fine_ends_kernel(cols, blocks, far_h, grid_in, side_in, change_in, out_in, *rest):
    fine_outer(cols, True, blocks, far_h, *rest)


def fine_outer(cols, sides, blocks, far_h, grid, side, change, out, far, *rest):
    *sends, iterate, sems = rest
    write_row(grid, far_h, -1, cols, far_is_inside())
    fine_second(0, cols, blocks, grid, side, change, iterate, 0, far)
    copies = [
        send_out(iterate, n, out, fine_cell(0, q), count, sems.at[k])
        for k, (n, q, count) in enumerate(stretches(cols))
    ]
    if sides:
        read_sides(change, *sends, BLOCK_X)
    for copy in copies:
        copy.wait()


def next_first(rho, cols, side, blocks, grid, far=None):
    for n, q in enumerate(cols):
        cell = place(rho, COARSE_X) * BLOCK_Y + q
        first = smoothed(blocks, cell, side[rho * BLOCK_Y + q])
        grid[spot(rho, q)] = split(first)
        if far is not None:
            far[n] = first


def left_pair(rho, cols, blocks, side, change, coarse_side, own_blocks, coarse_grid, far=None):
    for q in cols:
        upper = fine_left(2 * rho, q, blocks, side, change)
        coarse_side[rho * BLOCK_Y + q] = upper + fine_left(2 * rho + 1, q, blocks, side, change)
    for n, q in enumerate(cols):
        cell = place(rho, COARSE_X) * BLOCK_Y + q
        first = smoothed(own_blocks, cell, coarse_side[rho * BLOCK_Y + q])
        coarse_grid[spot(rho, q)] = split(first)
        if far is not None:
            far[n] = first


def left_middle_kernel(cols, blocks, side, own_blocks, far_h, change_in, change, coarse_side, coarse_grid, far):
    write_row(change, far_h, -1, cols, far_is_inside())
    left_pair(0, cols, blocks, side, change, coarse_side, own_blocks, coarse_grid, far)


def left_inner_kernel(
    blocks, side, own_blocks, near_h, even_h, odd_h, change_in, coarse_in, grid_in, change, coarse_side, coarse_grid
):
    write_row(change, near_h, BLOCK_X, range(BLOCK_Y))
    write_sides(change, even_h, odd_h, BLOCK_X)

    def body(rho, start):
        cols = [start + q for q in range(UNROLL)]
        left_pair(rho, cols, blocks, side, change, coarse_side, own_blocks, coarse_grid)

    over_rows(1, COARSE_X, body)


def left_ends_kernel(
    cols, blocks, side, own_blocks, far_h, change_in, coarse_in, grid_in, change, coarse_side, coarse_grid, far, *sends
):
    write_row(change, far_h, -1, cols, far_is_inside())
    left_pair(0, cols, blocks, side, change, coarse_side, own_blocks, coarse_grid, far)
    read_sides(coarse_grid, *sends, COARSE_X)


def own_blocks_kernel(diagonal, inverse, blocks):
    for cell in range(diagonal.shape[0]):
        blocks[cell] = jnp.concatenate([diagonal[cell], inverse[cell]], axis=1)


def near_blocks_kernel(coupling, after, blocks):
    species = coupling.shape[1]
    first = pl.program_id(0) * coupling.shape[0]
    for n in range(coupling.shape[0]):
        blocks[first + n] = coupling[n].reshape(species, 8 * species)


def coarse_apply(rho, q, places, blocks, own_blocks, grid):
    cell = place(rho, COARSE_X) * BLOCK_Y + q
    near = jnp.concatenate([grid[places[k, cell]] for k in range(8)], axis=0)
    return dot((blocks[cell], near), (own_blocks[cell], with_zeros(grid[spot(rho, q)], True)))


def coarse_second(rho, cols, places, blocks, own_blocks, grid, side, change, iterate, n, far=None):
    for q in cols:
        here = rho * BLOCK_Y + q
        side[here] = side[here] - coarse_apply(rho, q, places, blocks, own_blocks, grid)
    for m, q in enumerate(cols):
        here = spot(rho, q)
        step = smoothed(own_blocks, place(rho, COARSE_X) * BLOCK_Y + q, side[rho * BLOCK_Y + q])
        change[here] = split(step)
        iterate[n + m] = fold(grid[here]) + step
        if far is not None:
            far[m] = step


def pack_kernel(even_h, odd_h, grid_in, grid, corners, near):
    write_sides(grid, even_h, odd_h, COARSE_X)
    read_row(grid, corners, 0, (-1, BLOCK_Y))
    read_row(grid, near, COARSE_X - 1, range(-1, BLOCK_Y + 1))


def coarse_inner_kernel(
    places, blocks, own_blocks, near_h, grid_in, side_in, change_in, out_in, grid, side, change, out, iterate, sems
):
    write_row(grid, near_h, COARSE_X, range(-1, BLOCK_Y + 1))

    def body(rho, start):
        n = (rho - 1) * BLOCK_Y + start
        cell = place(rho, COARSE_X) * BLOCK_Y + start
        coarse_second(rho, [start + q for q in range(UNROLL)], places, blocks, own_blocks, grid, side, change, iterate, n)
        send_out(iterate, n, out, cell, UNROLL, sems.at[n // UNROLL])

    over_rows(1, COARSE_X, body)
    for n in range((COARSE_X - 1) * BLOCK_Y // UNROLL):
        part = iterate.at[pl.ds(n * UNROLL, UNROLL)]
        pltpu.make_async_copy(part, out.at[pl.ds(0, UNROLL)], sems.at[n]).wait()


def coarse_middle_kernel(came, cols, places, blocks, own_blocks, far_h, grid_in, side_in, *rest):
    coarse_outer(came, cols, False, places, blocks, own_blocks, far_h, *rest)


def coarse_ends_kernel(came, cols, places, blocks, own_blocks, far_h, corners_h, grid_in, side_in, change_in, out_in, grid, *rest):
    write_row(grid, corners_h, -1, (-1, BLOCK_Y))
    coarse_outer(came, cols, True, places, blocks, own_blocks, far_h, grid, *rest)


def coarse_outer(came, cols, sides, places, blocks, own_blocks, far_h, grid, side, change, out, far, *rest):
    *sends, iterate, sems = rest
    write_row(grid, far_h, -1, came)
    coarse_second(0, cols, places, blocks, own_blocks, grid, side, change, iterate, 0, far)
    copies = [
        send_out(iterate, n, out, place(0, COARSE_X) * BLOCK_Y + q, count, sems.at[k])
        for k, (n, q, count) in enumerate(stretches(cols))
    ]
    if sides:
        read_sides(change, *sends, COARSE_X)
    for copy in copies:
        copy.wait()


def coarse_left(rho, q, places, blocks, own_blocks, side, change):
    return side[rho * BLOCK_Y + q] - coarse_apply(rho, q, places, blocks, own_blocks, change)


def last_pair(rho, q, places, blocks, own_blocks, side, change):
    return coarse_left(rho, q, places, blocks, own_blocks, side, change) + coarse_left(rho, q + 1, places, blocks, own_blocks, side, change)


def last_inner_kernel(places, blocks, own_blocks, side, near_h, change_in, out_in, change, out, below, sems):
    write_row(change, near_h, COARSE_X, range(-1, BLOCK_Y + 1))
    count = UNROLL // 2

    def body(rho, start):
        n = ((rho - 1) * BLOCK_Y + start) // 2
        for q in range(count):
            below[n + q] = last_pair(rho, start + 2 * q, places, blocks, own_blocks, side, change)
        send_out(below, n, out, (place(rho, COARSE_X) * BLOCK_Y + start) // 2, count, sems.at[n // count])

    over_rows(1, COARSE_X, body)
    for n in range((COARSE_X - 1) * BLOCK_Y // UNROLL):
        part = below.at[pl.ds(n * count, count)]
        pltpu.make_async_copy(part, out.at[pl.ds(0, count)], sems.at[n]).wait()


def last_middle_kernel(came, cols, places, blocks, own_blocks, side, far_h, change_in, *rest):
    last_outer(came, cols, places, blocks, own_blocks, side, far_h, *rest)


def last_ends_kernel(came, cols, places, blocks, own_blocks, side, far_h, corners_h, change_in, out_in, change, *rest):
    write_row(change, corners_h, -1, (-1, BLOCK_Y))
    last_outer(came, cols, places, blocks, own_blocks, side, far_h, change, *rest)


def last_outer(came, cols, places, blocks, own_blocks, side, far_h, change, out, below, sems):
    write_row(change, far_h, -1, came)
    pairs = [q // 2 for q in cols[::2]]
    for n, q in enumerate(pairs):
        below[n] = last_pair(0, 2 * q, places, blocks, own_blocks, side, change)
    copies = [
        send_out(below, n, out, place(0, COARSE_X) * BLOCK_Y // 2 + q, count, sems.at[k])
        for k, (n, q, count) in enumerate(stretches(pairs))
    ]
    for copy in copies:
        copy.wait()


IN_VMEM = pl.BlockSpec(memory_space=pltpu.VMEM)
LONG = 10**11


def run(name, kernel, outs, args, aliases=(), smem=(), hbm=(), hbm_outs=(), smem_outs=(), scratch=(), after=(), cost=1):
    count = len(args)
    args = list(args) + list(after)
    spaces = [pltpu.SMEM if n in smem else pltpu.HBM if n in hbm else pltpu.VMEM for n in range(len(args))]
    out_spaces = [
        pltpu.SMEM if n in smem_outs else pltpu.HBM if n in hbm_outs else pltpu.VMEM for n in range(len(outs))
    ]

    def body(*refs):
        kernel(*refs[:count], *refs[len(args) :])

    called = pl.pallas_call(
        body,
        out_shape=tuple(space(shape, dtype) for space, (shape, dtype) in zip(out_spaces, outs)),
        in_specs=[pl.BlockSpec(memory_space=space) for space in spaces],
        out_specs=tuple(pl.BlockSpec(memory_space=space) for space in out_spaces),
        scratch_shapes=list(scratch),
        input_output_aliases=dict(aliases),
        compiler_params=pltpu.CompilerParams(vmem_limit_bytes=8 * 2**20),
        cost_estimate=pl.CostEstimate(flops=cost, bytes_accessed=1, transcendentals=0),
        name=name,
    )
    return called(*(pltpu.with_memory_space_constraint(x, space) for x, space in zip(args, spaces)))


def near_blocks_call(coupling, after):
    cells, species = coupling.shape[:2]
    part = cells // 8
    return pl.pallas_call(
        near_blocks_kernel,
        grid=(cells // part,),
        out_shape=pltpu.VMEM((cells, species, 8 * species), BF16),
        in_specs=[pl.BlockSpec((part,) + coupling.shape[1:], lambda n: (n, 0, 0, 0)), IN_VMEM],
        out_specs=IN_VMEM,
        compiler_params=pltpu.CompilerParams(vmem_limit_bytes=8 * 2**20),
        cost_estimate=pl.CostEstimate(flops=1, bytes_accessed=1, transcendentals=0),
        name="near_blocks",
    )(coupling, pltpu.with_memory_space_constraint(after, pltpu.VMEM))


def places_kernel(across, pattern, places, made, sem):
    number = pattern[...]
    per_block = COARSE_X * BLOCK_Y
    owner = lax.div(number, per_block)
    inside = lax.rem(number, per_block)
    row = lax.div(owner, across) * COARSE_X + lax.div(inside, BLOCK_Y) - lax.axis_index("gx") * COARSE_X
    col = lax.rem(owner, across) * BLOCK_Y + lax.rem(inside, BLOCK_Y) - lax.axis_index("gy") * BLOCK_Y
    rho = jnp.where(row_parity() == 0, row, COARSE_X - 1 - row)
    made[...] = (rho + 1) * WIDE + col + 1
    copy = pltpu.make_async_copy(made, places, sem)
    copy.start()
    copy.wait()


def on_device(
    right_side,
    fine_coupling,
    fine_diagonal,
    fine_inverse,
    coarse_coupling,
    coarse_diagonal,
    coarse_inverse,
    coarse_pattern,
):
    cells, species, vectors = right_side.shape
    coarse_cells = coarse_coupling.shape[0]
    rows, cols = lax.axis_size("gx"), lax.axis_size("gy")
    far_pairs, near_pairs = swap_far(rows, cols), swap_near(rows, cols)
    even_pairs, odd_pairs = swap_even(rows, cols), swap_odd(rows, cols)

    def far(x):
        return lax.ppermute(x, BOTH, far_pairs)

    def near(x):
        return lax.ppermute(x, BOTH, near_pairs)

    def even(x):
        return lax.ppermute(x, BOTH, even_pairs)

    def odd(x):
        return lax.ppermute(x, BOTH, odd_pairs)

    def field(count):
        return ((count, species, vectors), F32)

    def row_scratch(count):
        return [pltpu.VMEM((count, species, vectors), F32), pltpu.SemaphoreType.DMA((max(2, count // 8),))]

    def padded(count):
        return (((count + 2) * WIDE, species, 2 * vectors), BF16)

    fine_blocks = ((cells, species, 6 * species), BF16)
    coupling = jnp.transpose(fine_coupling, (1, 2, 3, 0)).reshape(species, 4 * species, cells)
    diagonal = jnp.transpose(fine_diagonal, (1, 2, 0))
    inverse = jnp.transpose(fine_inverse, (1, 2, 0))
    pattern = coarse_pattern.T
    middle, ends = len(MIDDLE), len(ENDS)

    blocks, grid, side, far_m, far_n = run(
        "start",
        start_kernel,
        [fine_blocks, padded(BLOCK_X), field(cells), field(middle), field(ends)],
        [right_side, inverse],
        hbm=(0, 1),
        scratch=[pltpu.VMEM(inverse.shape, BF16), pltpu.SemaphoreType.DMA((2 + BLOCK_X,))],
    )
    far_m, far_n = far(far_m), far(far_n)
    grid, near_s, even_s, odd_s = run(
        "first",
        first_kernel,
        [padded(BLOCK_X), field(BLOCK_Y), field(BLOCK_X), field(BLOCK_X)],
        [side, blocks, grid],
        [(2, 0)],
    )
    near_h, even_h, odd_h = near(near_s), even(even_s), odd(odd_s)
    (blocks,) = run(
        "fine_blocks",
        fine_blocks_kernel,
        [fine_blocks],
        [coupling, diagonal, inverse, blocks],
        [(3, 0)],
        after=[near_s],
    )
    state = [padded(BLOCK_X), field(cells), padded(BLOCK_X), field(cells)]
    grid, side, change, iterate, far_m = run(
        "fine_middle",
        functools.partial(fine_middle_kernel, MIDDLE),
        state + [field(middle)],
        [blocks, far_m, grid, side],
        [(2, 0), (3, 1)],
        hbm_outs=(3,),
        scratch=row_scratch(middle),
        after=[even_h, odd_h],
        cost=LONG,
    )
    far_m = far(far_m)
    grid, side, change, iterate, near_s = run(
        "fine_inner",
        fine_inner_kernel,
        state + [field(BLOCK_Y)],
        [blocks, near_h, even_h, odd_h, grid, side, change, iterate],
        [(4, 0), (5, 1), (6, 2), (7, 3)],
        hbm=(7,),
        hbm_outs=(3,),
        scratch=row_scratch((BLOCK_X - 1) * BLOCK_Y),
    )
    near_h = near(near_s)
    grid, side, change, fine_iterate, far_n, even_s, odd_s = run(
        "fine_ends",
        functools.partial(fine_ends_kernel, ENDS),
        state + [field(ends), field(BLOCK_X), field(BLOCK_X)],
        [blocks, far_n, grid, side, change, iterate],
        [(2, 0), (3, 1), (4, 2), (5, 3)],
        hbm=(5,),
        hbm_outs=(3,),
        scratch=row_scratch(ends),
    )
    (own_blocks,) = run(
        "own_blocks",
        own_blocks_kernel,
        [((coarse_cells, species, 2 * species), BF16)],
        [coarse_diagonal, coarse_inverse],
        after=[far_n],
    )
    far_n = far(far_n)
    even_h, odd_h = even(even_s), odd(odd_s)

    state = [padded(BLOCK_X), field(coarse_cells), padded(COARSE_X)]
    change, coarse_side, coarse_grid, far_m = run(
        "left_middle",
        functools.partial(left_middle_kernel, MIDDLE),
        state + [field(middle)],
        [blocks, side, own_blocks, far_m, change],
        [(4, 0)],
        after=[even_h, odd_h],
        cost=LONG,
    )
    far_m = far(far_m)
    change, coarse_side, coarse_grid = run(
        "left_inner",
        left_inner_kernel,
        state,
        [blocks, side, own_blocks, near_h, even_h, odd_h, change, coarse_side, coarse_grid],
        [(6, 0), (7, 1), (8, 2)],
    )
    change, coarse_side, coarse_grid, far_n, even_s, odd_s = run(
        "left_ends",
        functools.partial(left_ends_kernel, ENDS),
        state + [field(ends), field(COARSE_X), field(COARSE_X)],
        [blocks, side, own_blocks, far_n, change, coarse_side, coarse_grid],
        [(4, 0), (5, 1), (6, 2)],
    )
    near_blocks = near_blocks_call(coarse_coupling, far_n)
    (places,) = run(
        "places",
        functools.partial(places_kernel, cols),
        [(pattern.shape, jnp.int32)],
        [pattern],
        smem_outs=(0,),
        scratch=[pltpu.VMEM(pattern.shape, jnp.int32), pltpu.SemaphoreType.DMA],
        after=[near_blocks],
    )
    far_n = far(far_n)
    even_h, odd_h = even(even_s), odd(odd_s)
    coarse_grid, corners, near_s = run(
        "pack_first",
        pack_kernel,
        [padded(COARSE_X), field(2), field(BLOCK_Y + 2)],
        [even_h, odd_h, coarse_grid],
        [(2, 0)],
        after=[near_blocks],
    )
    corners, near_h = far(corners), near(near_s)

    state = [padded(COARSE_X), field(coarse_cells), padded(COARSE_X), field(coarse_cells)]
    inner = MIDDLE[1:-1]
    outer = tuple(q for q in range(BLOCK_Y) if q not in inner)
    coarse_grid, coarse_side, coarse_change, iterate, far_m = run(
        "coarse_middle",
        functools.partial(coarse_middle_kernel, MIDDLE, inner),
        state + [field(len(inner))],
        [places, near_blocks, own_blocks, far_m, coarse_grid, coarse_side],
        [(4, 0), (5, 1)],
        smem=(0,),
        hbm_outs=(3,),
        scratch=row_scratch(len(inner)),
        cost=LONG,
    )
    far_m = far(far_m)
    coarse_grid, coarse_side, coarse_change, iterate = run(
        "coarse_inner",
        coarse_inner_kernel,
        state,
        [places, near_blocks, own_blocks, near_h, coarse_grid, coarse_side, coarse_change, iterate],
        [(4, 0), (5, 1), (6, 2), (7, 3)],
        smem=(0,),
        hbm=(7,),
        hbm_outs=(3,),
        scratch=row_scratch((COARSE_X - 1) * BLOCK_Y),
    )
    coarse_grid, coarse_side, coarse_change, coarse_iterate, far_n, even_s, odd_s = run(
        "coarse_ends",
        functools.partial(coarse_ends_kernel, ENDS, outer),
        state + [field(len(outer)), field(COARSE_X), field(COARSE_X)],
        [places, near_blocks, own_blocks, far_n, corners, coarse_grid, coarse_side, coarse_change, iterate],
        [(5, 0), (6, 1), (7, 2), (8, 3)],
        smem=(0,),
        hbm=(8,),
        hbm_outs=(3,),
        scratch=row_scratch(len(outer)),
    )
    far_n = far(far_n)
    even_h, odd_h = even(even_s), odd(odd_s)
    coarse_change, corners, near_s = run(
        "pack_second",
        pack_kernel,
        [padded(COARSE_X), field(2), field(BLOCK_Y + 2)],
        [even_h, odd_h, coarse_change],
        [(2, 0)],
    )
    corners, near_h = far(corners), near(near_s)

    state = [padded(COARSE_X), field(coarse_cells // 2)]
    core = inner[1:-1]
    rest = tuple(q for q in range(BLOCK_Y) if q not in core)
    coarse_change, next_side = run(
        "last_middle",
        functools.partial(last_middle_kernel, inner, core),
        state,
        [places, near_blocks, own_blocks, coarse_side, far_m, coarse_change],
        [(5, 0)],
        smem=(0,),
        hbm_outs=(1,),
        scratch=row_scratch(len(core) // 2),
        cost=LONG,
    )
    coarse_change, next_side = run(
        "last_inner",
        last_inner_kernel,
        state,
        [places, near_blocks, own_blocks, coarse_side, near_h, coarse_change, next_side],
        [(5, 0), (6, 1)],
        smem=(0,),
        hbm=(6,),
        hbm_outs=(1,),
        scratch=row_scratch((COARSE_X - 1) * BLOCK_Y // 2),
    )
    coarse_change, next_side = run(
        "last_ends",
        functools.partial(last_ends_kernel, outer, rest),
        state,
        [places, near_blocks, own_blocks, coarse_side, far_n, corners, coarse_change, next_side],
        [(6, 0), (7, 1)],
        smem=(0,),
        hbm=(7,),
        hbm_outs=(1,),
        scratch=row_scratch(len(rest) // 2),
    )
    return (fine_iterate, coarse_iterate, next_side)


def solution(mesh):
    placed = (
        P(BOTH, None, None),
        P(BOTH, None, None, None),
        P(BOTH, None, None),
        P(BOTH, None, None),
        P(BOTH, None, None, None),
        P(BOTH, None, None),
        P(BOTH, None, None),
        P(BOTH, None),
    )
    return jax.shard_map(
        on_device,
        mesh=mesh,
        in_specs=placed,
        out_specs=(P(BOTH, None, None), P(BOTH, None, None), P(BOTH, None, None)),
        check_vma=False,
    )
```

```python
import functools

import jax
import jax.numpy as jnp
from jax import lax
from jax.experimental import pallas as pl
from jax.experimental.pallas import tpu as pltpu
from jax.sharding import PartitionSpec as P

BLOCK_X = 4
BLOCK_Y = 32

WIDE = BLOCK_Y + 2
COARSE_X = BLOCK_X // 2
EDGE = BLOCK_Y // 4
MIDDLE = tuple(range(EDGE, BLOCK_Y - EDGE))
ENDS = tuple(q for q in range(BLOCK_Y) if q not in MIDDLE)
SIDES = (0, BLOCK_Y - 1)
BESIDE = (-1, BLOCK_Y)
INSIDE = tuple(range(1, BLOCK_Y - 1))

F32 = jnp.float32
BF16 = jnp.bfloat16
BOTH = ("gx", "gy")


def split(x):
    high = x.astype(BF16)
    low = (x - high.astype(F32)).astype(BF16)
    return jnp.concatenate([high, low], axis=1)


def fold(x):
    half = x.shape[1] // 2
    return x[:, :half].astype(F32) + x[:, half:].astype(F32)


def dot(*pairs):
    parts = [jnp.dot(a, b, preferred_element_type=F32) for a, b in pairs]
    return fold(functools.reduce(jnp.add, parts))


def row_parity():
    return lax.rem(lax.axis_index("gx"), 2)


def col_parity():
    return lax.rem(lax.axis_index("gy"), 2)


def place(rho, rows):
    parity = row_parity()
    return rho + parity * (rows - 1 - 2 * rho)


def spot(rho, q):
    return (rho + 1) * WIDE + q + 1


def swap_far(rows, cols, hop):
    pairs = []
    for a in range(rows):
        for b in range(cols):
            partner = a - 1 if a % 2 == 0 else a + 1
            if 0 <= partner < rows:
                pairs.append((a * cols + b, partner * cols + b))
            else:
                pairs.append((a * cols + b, a * cols + (b ^ hop)))
    return pairs


def swap_near(rows, cols):
    return [(a * cols + b, (a ^ 1) * cols + b) for a in range(rows) for b in range(cols)]


def swap_even(rows, cols):
    return [(a * cols + b, a * cols + (b ^ 1)) for a in range(rows) for b in range(cols)]


def swap_odd(rows, cols):
    pairs = []
    for a in range(rows):
        for b in range(cols):
            partner = b - 1 if b % 2 == 0 else b + 1
            if 0 <= partner < cols:
                pairs.append((a * cols + b, a * cols + partner))
            else:
                pairs.append((a * cols + b, (a ^ 1) * cols + b))
    return pairs


def far_is_inside():
    gx = lax.axis_index("gx")
    return jnp.where(row_parity() == 0, gx > 0, gx < lax.axis_size("gx") - 1)


def odd_is_inside():
    gy = lax.axis_index("gy")
    return jnp.where(col_parity() == 0, gy > 0, gy < lax.axis_size("gy") - 1)


def write_sides(grid, even_halo, odd_halo, rows):
    parity = col_parity()
    even_col = jnp.where(parity == 0, BLOCK_Y, -1)
    odd_col = BLOCK_Y - 1 - even_col
    inside = odd_is_inside()
    for rho in range(rows):
        grid[spot(rho, even_col)] = split(even_halo[rho])
        grid[spot(rho, odd_col)] = split(jnp.where(inside, odd_halo[rho], 0.0))


def read_sides(grid, even_send, odd_send, rows):
    parity = col_parity()
    even_col = jnp.where(parity == 0, BLOCK_Y - 1, 0)
    odd_col = BLOCK_Y - 1 - even_col
    for rho in range(rows):
        even_send[rho] = fold(grid[spot(rho, even_col)])
        odd_send[rho] = fold(grid[spot(rho, odd_col)])


def write_row(grid, halo, rho, cols, inside=None):
    for n, q in enumerate(cols):
        value = halo[n]
        if inside is not None:
            value = jnp.where(inside, value, 0.0)
        grid[spot(rho, q)] = split(value)


def read_row(grid, send, rho, cols):
    for n, q in enumerate(cols):
        send[n] = fold(grid[spot(rho, q)])


def over_rows(first, last, body):
    def step(rho, carry):
        body(rho)
        return carry

    lax.fori_loop(first, last, step, 0)


def stretches(cols):
    found = []
    for n, q in enumerate(cols):
        if found and found[-1][1] + found[-1][2] == q:
            found[-1][2] += 1
        else:
            found.append([n, q, 1])
    return found


def with_zeros(own, after):
    none = jnp.zeros(own.shape, BF16)
    return jnp.concatenate([own, none] if after else [none, own], axis=0)


def smoothed(blocks, cell, side):
    species = side.shape[0]
    return dot((blocks[cell, :, -2 * species :], with_zeros(split(side), False)))


def fine_cell(rho, q):
    return place(rho, BLOCK_X) * BLOCK_Y + q


def fine_apply(rho, q, blocks, grid):
    cell = fine_cell(rho, q)
    species = blocks.shape[1]
    here = spot(rho, q)
    step = WIDE * (1 - 2 * row_parity())
    near = jnp.concatenate([grid[here - step], grid[here + step], grid[here - 1], grid[here + 1]], axis=0)
    return dot(
        (blocks[cell, :, : 4 * species], near), (blocks[cell, :, 4 * species :], with_zeros(grid[here], True))
    )


def fine_second(rho, cols, blocks, grid, side, change, iterate, first, far=None):
    for q in cols:
        cell = fine_cell(rho, q)
        side[cell] = side[cell] - fine_apply(rho, q, blocks, grid)
    for m, q in enumerate(cols):
        cell = fine_cell(rho, q)
        here = spot(rho, q)
        step = smoothed(blocks, cell, side[cell])
        change[here] = split(step)
        iterate[first + q] = fold(grid[here]) + step
        if far is not None:
            far[m] = step


def fine_left(rho, q, blocks, side, change):
    return side[fine_cell(rho, q)] - fine_apply(rho, q, blocks, change)


def start_kernel(right, inverse, blocks, grid, side, far_m, far_n, inverse_here, sems):
    species = inverse.shape[0]
    part = species // 2
    loads = [
        pltpu.make_async_copy(inverse.at[pl.ds(n * part, part)], inverse_here.at[pl.ds(n * part, part)], sems.at[n])
        for n in range(2)
    ]
    for rho in range(BLOCK_X):
        row = pl.ds(fine_cell(rho, 0), BLOCK_Y)
        loads.append(pltpu.make_async_copy(right.at[row], side.at[row], sems.at[2 + rho]))
    for load in loads:
        load.start()
    for n in range(2):
        loads[n].wait()
        some = inverse_here[n * part : (n + 1) * part]
        both = jnp.concatenate([jnp.zeros(some.shape, BF16), some], axis=1)
        blocks[:, n * part : (n + 1) * part, 4 * species :] = jnp.transpose(both, (2, 0, 1))
    loads[2].wait()
    for cols, send in ((MIDDLE, far_m), (ENDS, far_n)):
        for n, q in enumerate(cols):
            cell = fine_cell(0, q)
            first = smoothed(blocks, cell, side[cell])
            grid[spot(0, q)] = split(first)
            send[n] = first
    for load in loads[3:]:
        load.wait()


def first_kernel(side, blocks, grid_in, grid, near, even, odd):
    def row(rho, near=None):
        for q in range(BLOCK_Y):
            cell = fine_cell(rho, q)
            first = smoothed(blocks, cell, side[cell])
            grid[spot(rho, q)] = split(first)
            if near is not None:
                near[q] = first

    over_rows(1, BLOCK_X - 1, row)
    row(BLOCK_X - 1, near)
    read_sides(grid, even, odd, BLOCK_X)


def fine_blocks_kernel(coupling, diagonal, inverse, blocks_in, blocks):
    species = coupling.shape[0]
    part = species // 2
    for first in range(0, species, part):
        rows = slice(first, first + part)
        blocks[:, rows, : 4 * species] = jnp.transpose(coupling[rows], (2, 0, 1))
        both = jnp.concatenate([diagonal[rows], inverse[rows]], axis=1)
        blocks[:, rows, 4 * species :] = jnp.transpose(both, (2, 0, 1))


def fine_inner_kernel(
    blocks, near_h, even_h, odd_h, grid_in, side_in, change_in, grid, side, change, out, last, near, made, sems
):
    write_row(grid, near_h, BLOCK_X, range(BLOCK_Y))
    write_sides(grid, even_h, odd_h, BLOCK_X)

    def leave(rho):
        source = made.at[pl.ds((rho - 1) * BLOCK_Y, BLOCK_Y)]
        return pltpu.make_async_copy(source, out.at[pl.ds(fine_cell(rho, 0), BLOCK_Y)], sems.at[rho - 1])

    def body(rho):
        fine_second(rho, range(BLOCK_Y), blocks, grid, side, change, made, (rho - 1) * BLOCK_Y)
        leave(rho).start()

    over_rows(1, BLOCK_X - 1, body)
    fine_second(BLOCK_X - 1, range(BLOCK_Y), blocks, grid, side, change, last, 0, near)
    for rho in range(1, BLOCK_X - 1):
        leave(rho).wait()


def fine_middle_kernel(cols, blocks, far_h, grid_in, side_in, grid, side, change, iterate, far):
    write_row(grid, far_h, -1, cols, far_is_inside())
    fine_second(0, cols, blocks, grid, side, change, iterate, 0, far)


def fine_ends_kernel(
    cols, blocks, far_h, grid_in, side_in, change_in, iterate_in, grid, side, change, iterate, far, even, odd
):
    write_row(grid, far_h, -1, cols, far_is_inside())
    fine_second(0, cols, blocks, grid, side, change, iterate, 0, far)
    read_sides(change, even, odd, BLOCK_X)


def left_pair(rho, cols, blocks, side, change, coarse_side, own_blocks, coarse_grid, far=None, shift=0):
    for q in cols:
        upper = fine_left(2 * rho, q, blocks, side, change)
        coarse_side[rho * BLOCK_Y + q] = upper + fine_left(2 * rho + 1, q, blocks, side, change)
    for n, q in enumerate(cols):
        cell = place(rho, COARSE_X) * BLOCK_Y + q
        first = smoothed(own_blocks, cell, coarse_side[rho * BLOCK_Y + q])
        coarse_grid[spot(rho, q)] = split(first)
        if far is not None:
            far[n + shift] = first


def left_middle_kernel(cols, blocks, side, own_blocks, far_h, change_in, change, coarse_side, coarse_grid, far):
    write_row(change, far_h, -1, cols, far_is_inside())
    left_pair(0, cols, blocks, side, change, coarse_side, own_blocks, coarse_grid, far)


def left_ends_kernel(
    cols,
    blocks,
    side,
    own_blocks,
    far_h,
    near_h,
    even_h,
    odd_h,
    change_in,
    coarse_in,
    grid_in,
    change,
    coarse_side,
    coarse_grid,
    far,
    even,
    odd,
):
    write_row(change, far_h, -1, cols, far_is_inside())
    write_row(change, near_h, BLOCK_X, range(BLOCK_Y))
    write_sides(change, even_h, odd_h, BLOCK_X)
    left_pair(0, cols, blocks, side, change, coarse_side, own_blocks, coarse_grid, far)
    for rho in range(1, COARSE_X):
        left_pair(rho, SIDES, blocks, side, change, coarse_side, own_blocks, coarse_grid)
    read_sides(coarse_grid, even, odd, COARSE_X)


def left_inner_kernel(blocks, side, own_blocks, change, coarse_in, grid_in, coarse_side, coarse_grid, near):
    for rho in range(1, COARSE_X):
        last = near if rho == COARSE_X - 1 else None
        left_pair(rho, INSIDE, blocks, side, change, coarse_side, own_blocks, coarse_grid, last, INSIDE[0])
    for q in SIDES:
        near[q] = fold(coarse_grid[spot(COARSE_X - 1, q)])


def near_blocks_kernel(coupling, first_row, last_row, out_in, blocks, out, sems):
    species = coupling.shape[1]
    step, count = pl.program_id(0), coupling.shape[0]
    copies = []
    for n, (rho, source) in enumerate(((0, first_row), (BLOCK_X - 1, last_row))):
        target = out.at[pl.ds(fine_cell(rho, 0), BLOCK_Y)]
        copies.append(pltpu.make_async_copy(source, target, sems.at[n]))

    @pl.when(step == 0)
    def _():
        for copy in copies:
            copy.start()

    for n in range(count):
        blocks[step * count + n] = coupling[n].reshape(species, 8 * species)

    @pl.when(step == pl.num_programs(0) - 1)
    def _():
        for copy in copies:
            copy.wait()


def coarse_apply(rho, q, places, blocks, own_blocks, grid):
    cell = place(rho, COARSE_X) * BLOCK_Y + q
    near = jnp.concatenate([grid[places[k, cell]] for k in range(8)], axis=0)
    return dot((blocks[cell], near), (own_blocks[cell], with_zeros(grid[spot(rho, q)], True)))


def coarse_second(rho, cols, places, blocks, own_blocks, grid, side, change, iterate, far=None, shift=0):
    for q in cols:
        here = rho * BLOCK_Y + q
        side[here] = side[here] - coarse_apply(rho, q, places, blocks, own_blocks, grid)
    for m, q in enumerate(cols):
        here = spot(rho, q)
        cell = place(rho, COARSE_X) * BLOCK_Y + q
        step = smoothed(own_blocks, cell, side[rho * BLOCK_Y + q])
        change[here] = split(step)
        iterate[cell] = fold(grid[here]) + step
        if far is not None:
            far[m + shift] = step


def pack_kernel(even_h, odd_h, grid_in, grid, far, near):
    write_sides(grid, even_h, odd_h, COARSE_X)
    read_row(grid, far, 0, BESIDE)
    read_row(grid, near, COARSE_X - 1, BESIDE)


def row_out(source, out, rho, sem):
    some = pl.ds(place(rho, COARSE_X) * BLOCK_Y, BLOCK_Y)
    return pltpu.make_async_copy(source.at[some], out.at[some], sem)


def coarse_inner_kernel(
    places, blocks, own_blocks, grid, side_in, change_in, iterate_in, side, change, iterate, near, out, sem
):
    leave = row_out(iterate, out, 0, sem)
    leave.start()
    for rho in range(1, COARSE_X):
        last = near if rho == COARSE_X - 1 else None
        coarse_second(rho, INSIDE, places, blocks, own_blocks, grid, side, change, iterate, last, INSIDE[0])
    for q in SIDES:
        near[q] = fold(change[spot(COARSE_X - 1, q)])
    leave.wait()


def coarse_middle_kernel(
    came, cols, places, blocks, own_blocks, far_h, grid_in, side_in, grid, side, change, iterate, far
):
    write_row(grid, far_h, -1, came)
    coarse_second(0, cols, places, blocks, own_blocks, grid, side, change, iterate, far)


def coarse_ends_kernel(
    came,
    cols,
    places,
    blocks,
    own_blocks,
    far_h,
    corners_h,
    near_h,
    beside_h,
    grid_in,
    side_in,
    change_in,
    iterate_in,
    grid,
    side,
    change,
    iterate,
    far,
    even,
    odd,
):
    write_row(grid, far_h, -1, came)
    write_row(grid, corners_h, -1, BESIDE)
    write_row(grid, near_h, COARSE_X, range(BLOCK_Y))
    write_row(grid, beside_h, COARSE_X, BESIDE)
    coarse_second(0, cols, places, blocks, own_blocks, grid, side, change, iterate, far)
    for rho in range(1, COARSE_X):
        coarse_second(rho, SIDES, places, blocks, own_blocks, grid, side, change, iterate)
    read_sides(change, even, odd, COARSE_X)


def last_pairs(rho, pairs, places, blocks, own_blocks, side, change, below):
    first = place(rho, COARSE_X) * (BLOCK_Y // 2)
    for pair in pairs:
        q = 2 * pair
        total = side[rho * BLOCK_Y + q] + side[rho * BLOCK_Y + q + 1]
        total = total - coarse_apply(rho, q, places, blocks, own_blocks, change)
        total = total - coarse_apply(rho, q + 1, places, blocks, own_blocks, change)
        below[first + pair] = total


def last_middle_kernel(came, pairs, places, blocks, own_blocks, side, far_h, change_in, change, below):
    write_row(change, far_h, -1, came)
    last_pairs(0, pairs, places, blocks, own_blocks, side, change, below)


def last_inner_kernel(
    pairs, places, blocks, own_blocks, side, near_h, iterate, change_in, below_in, out_in, change, below, out, sems
):
    leave = [row_out(iterate, out, rho, sems.at[rho]) for rho in range(1, COARSE_X)]
    for copy in leave:
        copy.start()
    write_row(change, near_h, COARSE_X, range(BLOCK_Y))
    for rho in range(1, COARSE_X):
        last_pairs(rho, pairs, places, blocks, own_blocks, side, change, below)
    for copy in leave:
        copy.wait()


def last_ends_kernel(
    came,
    done,
    todo,
    places,
    blocks,
    own_blocks,
    side,
    far_h,
    corners_h,
    beside_h,
    change_in,
    below,
    change,
    out,
    made,
    sems,
):
    copies = []

    def send(source, rho, first, count):
        some = pl.ds(place(rho, COARSE_X) * (BLOCK_Y // 2) + first, count)
        copies.append(pltpu.make_async_copy(source.at[some], out.at[some], sems.at[len(copies)]))
        copies[-1].start()

    for rho in range(COARSE_X):
        for _, first, count in stretches(done[rho]):
            send(below, rho, first, count)
    write_row(change, far_h, -1, came)
    write_row(change, corners_h, -1, BESIDE)
    write_row(change, beside_h, COARSE_X, BESIDE)
    for rho in reversed(range(COARSE_X)):
        for _, first, count in stretches(todo[rho]):
            last_pairs(rho, range(first, first + count), places, blocks, own_blocks, side, change, made)
            send(made, rho, first, count)
    for copy in copies:
        copy.wait()


IN_VMEM = pl.BlockSpec(memory_space=pltpu.VMEM)
IN_HBM = pl.BlockSpec(memory_space=pltpu.HBM)
LONG = 10**11


def run(name, kernel, outs, args, aliases=(), smem=(), hbm=(), hbm_outs=(), smem_outs=(), scratch=(), after=(), cost=1, room=2):
    count = len(args)
    args = list(args) + list(after)
    spaces = [pltpu.SMEM if n in smem else pltpu.HBM if n in hbm else pltpu.VMEM for n in range(len(args))]
    out_spaces = [
        pltpu.SMEM if n in smem_outs else pltpu.HBM if n in hbm_outs else pltpu.VMEM for n in range(len(outs))
    ]

    def body(*refs):
        kernel(*refs[:count], *refs[len(args) :])

    called = pl.pallas_call(
        body,
        out_shape=tuple(space(shape, dtype) for space, (shape, dtype) in zip(out_spaces, outs)),
        in_specs=[pl.BlockSpec(memory_space=space) for space in spaces],
        out_specs=tuple(pl.BlockSpec(memory_space=space) for space in out_spaces),
        scratch_shapes=list(scratch),
        input_output_aliases=dict(aliases),
        compiler_params=pltpu.CompilerParams(vmem_limit_bytes=room * 2**20),
        cost_estimate=pl.CostEstimate(flops=cost, bytes_accessed=1, transcendentals=0),
        name=name,
    )
    return called(*(pltpu.with_memory_space_constraint(x, space) for x, space in zip(args, spaces)))


def near_blocks_call(coupling, first_row, last_row, out):
    cells, species = coupling.shape[:2]
    part = cells // 8
    here = [pltpu.with_memory_space_constraint(x, pltpu.VMEM) for x in (first_row, last_row)]
    return pl.pallas_call(
        near_blocks_kernel,
        grid=(cells // part,),
        out_shape=(pltpu.VMEM((cells, species, 8 * species), BF16), pltpu.HBM(out.shape, out.dtype)),
        in_specs=[
            pl.BlockSpec((part,) + coupling.shape[1:], lambda n: (n, 0, 0, 0)),
            IN_VMEM,
            IN_VMEM,
            IN_HBM,
        ],
        out_specs=(IN_VMEM, IN_HBM),
        scratch_shapes=[pltpu.SemaphoreType.DMA((2,))],
        input_output_aliases={3: 1},
        compiler_params=pltpu.CompilerParams(vmem_limit_bytes=5 * 2**20),
        cost_estimate=pl.CostEstimate(flops=1, bytes_accessed=1, transcendentals=0),
        name="near_blocks",
    )(coupling, *here, pltpu.with_memory_space_constraint(out, pltpu.HBM))


def own_blocks_kernel(across, diagonal, inverse, pattern, blocks, places, made, sem):
    number = pattern[...]
    per_block = COARSE_X * BLOCK_Y
    owner = lax.div(number, per_block)
    inside = lax.rem(number, per_block)
    row = lax.div(owner, across) * COARSE_X + lax.div(inside, BLOCK_Y) - lax.axis_index("gx") * COARSE_X
    col = lax.rem(owner, across) * BLOCK_Y + lax.rem(inside, BLOCK_Y) - lax.axis_index("gy") * BLOCK_Y
    rho = jnp.where(row_parity() == 0, row, COARSE_X - 1 - row)
    made[...] = (rho + 1) * WIDE + col + 1
    copy = pltpu.make_async_copy(made, places, sem)
    copy.start()
    for cell in range(diagonal.shape[0]):
        blocks[cell] = jnp.concatenate([diagonal[cell], inverse[cell]], axis=1)
    copy.wait()


def on_device(
    right_side,
    fine_coupling,
    fine_diagonal,
    fine_inverse,
    coarse_coupling,
    coarse_diagonal,
    coarse_inverse,
    coarse_pattern,
):
    cells, species, vectors = right_side.shape
    coarse_cells = coarse_coupling.shape[0]
    rows, cols = lax.axis_size("gx"), lax.axis_size("gy")
    far_pairs, near_pairs = swap_far(rows, cols, 2 if cols % 4 == 0 else 1), swap_near(rows, cols)
    corner_pairs = swap_far(rows, cols, 1)
    even_pairs, odd_pairs = swap_even(rows, cols), swap_odd(rows, cols)

    def far(x):
        return lax.ppermute(x, BOTH, far_pairs)

    def near(x):
        return lax.ppermute(x, BOTH, near_pairs)

    def even(x):
        return lax.ppermute(x, BOTH, even_pairs)

    def odd(x):
        return lax.ppermute(x, BOTH, odd_pairs)

    def field(count):
        return ((count, species, vectors), F32)

    def padded(count):
        return (((count + 2) * WIDE, species, 2 * vectors), BF16)

    fine_blocks = ((cells, species, 6 * species), BF16)
    coupling = jnp.transpose(fine_coupling, (1, 2, 3, 0)).reshape(species, 4 * species, cells)
    diagonal = jnp.transpose(fine_diagonal, (1, 2, 0))
    inverse = jnp.transpose(fine_inverse, (1, 2, 0))
    pattern = coarse_pattern.T
    middle, ends = len(MIDDLE), len(ENDS)

    blocks, grid, side, far_m, far_n = run(
        "start",
        start_kernel,
        [fine_blocks, padded(BLOCK_X), field(cells), field(middle), field(ends)],
        [right_side, inverse],
        hbm=(0, 1),
        scratch=[pltpu.VMEM(inverse.shape, BF16), pltpu.SemaphoreType.DMA((2 + BLOCK_X,))],
        room=6,
    )
    far_m, far_n = far(far_m), far(far_n)
    grid, near_s, even_s, odd_s = run(
        "first",
        first_kernel,
        [padded(BLOCK_X), field(BLOCK_Y), field(BLOCK_X), field(BLOCK_X)],
        [side, blocks, grid],
        [(2, 0)],
    )
    near_h, even_h, odd_h = near(near_s), even(even_s), odd(odd_s)
    (blocks,) = run(
        "fine_blocks",
        fine_blocks_kernel,
        [fine_blocks],
        [coupling, diagonal, inverse, blocks],
        [(3, 0)],
        after=[near_s],
        room=6,
    )
    own_blocks, places = run(
        "own_blocks",
        functools.partial(own_blocks_kernel, cols),
        [((coarse_cells, species, 2 * species), BF16), (pattern.shape, jnp.int32)],
        [coarse_diagonal, coarse_inverse, pattern],
        smem_outs=(1,),
        scratch=[pltpu.VMEM(pattern.shape, jnp.int32), pltpu.SemaphoreType.DMA],
        after=[blocks],
    )
    state = [padded(BLOCK_X), field(cells), padded(BLOCK_X)]
    grid, side, change, iterate, far_m = run(
        "fine_middle",
        functools.partial(fine_middle_kernel, MIDDLE),
        state + [field(BLOCK_Y), field(middle)],
        [blocks, far_m, grid, side],
        [(2, 0), (3, 1)],
        after=[even_h, odd_h, own_blocks],
        cost=LONG,
    )
    far_m = far(far_m)
    grid, side, change, fine_iterate, last_row, near_s = run(
        "fine_inner",
        fine_inner_kernel,
        state + [field(cells), field(BLOCK_Y), field(BLOCK_Y)],
        [blocks, near_h, even_h, odd_h, grid, side, change],
        [(4, 0), (5, 1), (6, 2)],
        hbm_outs=(3,),
        scratch=[
            pltpu.VMEM(((BLOCK_X - 2) * BLOCK_Y, species, vectors), F32),
            pltpu.SemaphoreType.DMA((BLOCK_X - 2,)),
        ],
        room=4,
    )
    near_h = near(near_s)
    grid, side, change, iterate, far_n, even_s, odd_s = run(
        "fine_ends",
        functools.partial(fine_ends_kernel, ENDS),
        state + [field(BLOCK_Y), field(ends), field(BLOCK_X), field(BLOCK_X)],
        [blocks, far_n, grid, side, change, iterate],
        [(2, 0), (3, 1), (4, 2), (5, 3)],
    )
    near_blocks, fine_iterate = near_blocks_call(coarse_coupling, iterate, last_row, fine_iterate)
    far_n = far(far_n)
    even_h, odd_h = even(even_s), odd(odd_s)

    state = [padded(BLOCK_X), field(coarse_cells), padded(COARSE_X)]
    change, coarse_side, coarse_grid, far_m = run(
        "left_middle",
        functools.partial(left_middle_kernel, MIDDLE),
        state + [field(middle)],
        [blocks, side, own_blocks, far_m, change],
        [(4, 0)],
        after=[even_h, odd_h, near_blocks],
        cost=LONG,
    )
    far_m = far(far_m)
    change, coarse_side, coarse_grid, far_n, even_s, odd_s = run(
        "left_ends",
        functools.partial(left_ends_kernel, ENDS),
        state + [field(ends), field(COARSE_X), field(COARSE_X)],
        [blocks, side, own_blocks, far_n, near_h, even_h, odd_h, change, coarse_side, coarse_grid],
        [(7, 0), (8, 1), (9, 2)],
        cost=LONG,
    )
    coarse_side, coarse_grid, near_s = run(
        "left_inner",
        left_inner_kernel,
        state[1:] + [field(BLOCK_Y)],
        [blocks, side, own_blocks, change, coarse_side, coarse_grid],
        [(4, 0), (5, 1)],
    )
    far_n = far(far_n)
    even_h, odd_h = even(even_s), odd(odd_s)
    near_h = near(near_s)
    coarse_grid, corners, beside = run(
        "pack_first",
        pack_kernel,
        [padded(COARSE_X), field(2), field(2)],
        [even_h, odd_h, coarse_grid],
        [(2, 0)],
    )
    corners, beside = lax.ppermute(corners, BOTH, corner_pairs), near(beside)

    state = [padded(COARSE_X), field(coarse_cells), padded(COARSE_X), field(coarse_cells)]
    inner = MIDDLE[1:-1]
    outer = tuple(q for q in range(BLOCK_Y) if q not in inner)
    coarse_grid, coarse_side, coarse_change, iterate, far_m = run(
        "coarse_middle",
        functools.partial(coarse_middle_kernel, MIDDLE, inner),
        state + [field(len(inner))],
        [places, near_blocks, own_blocks, far_m, coarse_grid, coarse_side],
        [(4, 0), (5, 1)],
        smem=(0,),
        cost=LONG,
    )
    far_m = far(far_m)
    coarse_grid, coarse_side, coarse_change, iterate, far_n, even_s, odd_s = run(
        "coarse_ends",
        functools.partial(coarse_ends_kernel, ENDS, outer),
        state + [field(len(outer)), field(COARSE_X), field(COARSE_X)],
        [places, near_blocks, own_blocks, far_n, corners, near_h, beside]
        + [coarse_grid, coarse_side, coarse_change, iterate],
        [(7, 0), (8, 1), (9, 2), (10, 3)],
        smem=(0,),
        cost=LONG,
    )
    coarse_side, coarse_change, iterate, near_s, coarse_iterate = run(
        "coarse_inner",
        coarse_inner_kernel,
        state[1:] + [field(BLOCK_Y), field(coarse_cells)],
        [places, near_blocks, own_blocks, coarse_grid, coarse_side, coarse_change, iterate],
        [(4, 0), (5, 1), (6, 2)],
        smem=(0,),
        hbm_outs=(4,),
        scratch=[pltpu.SemaphoreType.DMA],
    )
    far_n = far(far_n)
    even_h, odd_h = even(even_s), odd(odd_s)
    near_h = near(near_s)
    coarse_change, corners, beside = run(
        "pack_second",
        pack_kernel,
        [padded(COARSE_X), field(2), field(2)],
        [even_h, odd_h, coarse_change],
        [(2, 0)],
    )
    corners, beside = lax.ppermute(corners, BOTH, corner_pairs), near(beside)

    state = [padded(COARSE_X), field(coarse_cells // 2)]
    half = BLOCK_Y // 2
    core = tuple(q // 2 for q in inner[1:-1:2])
    pairs = tuple(range(1, half - 1))
    todo = [tuple(q for q in range(half) if q not in core)] + [(0, half - 1)] * (COARSE_X - 1)
    coarse_change, below = run(
        "last_middle",
        functools.partial(last_middle_kernel, inner, core),
        state,
        [places, near_blocks, own_blocks, coarse_side, far_m, coarse_change],
        [(5, 0)],
        smem=(0,),
        cost=LONG,
    )
    coarse_change, below, coarse_iterate = run(
        "last_inner",
        functools.partial(last_inner_kernel, pairs),
        state + [field(coarse_cells)],
        [places, near_blocks, own_blocks, coarse_side, near_h, iterate, coarse_change, below, coarse_iterate],
        [(6, 0), (7, 1), (8, 2)],
        smem=(0,),
        hbm=(8,),
        hbm_outs=(2,),
        scratch=[pltpu.SemaphoreType.DMA((COARSE_X,))],
    )
    coarse_change, next_side = run(
        "last_ends",
        functools.partial(last_ends_kernel, outer, [core] + [pairs] * (COARSE_X - 1), todo),
        state,
        [places, near_blocks, own_blocks, coarse_side, far_n, corners, beside, coarse_change, below],
        [(7, 0)],
        smem=(0,),
        hbm_outs=(1,),
        scratch=[pltpu.VMEM(state[1][0], F32), pltpu.SemaphoreType.DMA((4 * COARSE_X,))],
        room=3,
    )
    return (fine_iterate, coarse_iterate, next_side)


def solution(mesh):
    placed = (
        P(BOTH, None, None),
        P(BOTH, None, None, None),
        P(BOTH, None, None),
        P(BOTH, None, None),
        P(BOTH, None, None, None),
        P(BOTH, None, None),
        P(BOTH, None, None),
        P(BOTH, None),
    )
    return jax.shard_map(
        on_device,
        mesh=mesh,
        in_specs=placed,
        out_specs=(P(BOTH, None, None), P(BOTH, None, None), P(BOTH, None, None)),
        check_vma=False,
    )
```

```python
import functools

import jax
import jax.numpy as jnp
from jax import lax
from jax.experimental import pallas as pl
from jax.experimental.pallas import tpu as pltpu
from jax.sharding import PartitionSpec as P

BLOCK_X = 4
BLOCK_Y = 32

WIDE = BLOCK_Y + 2
COARSE_X = BLOCK_X // 2
EDGE = BLOCK_Y // 4
MIDDLE = tuple(range(EDGE, BLOCK_Y - EDGE))
ENDS = tuple(q for q in range(BLOCK_Y) if q not in MIDDLE)
SIDES = (0, BLOCK_Y - 1)
BESIDE = (-1, BLOCK_Y)
INSIDE = tuple(range(1, BLOCK_Y - 1))

F32 = jnp.float32
BF16 = jnp.bfloat16
BOTH = ("gx", "gy")


def split(x):
    high = x.astype(BF16)
    low = (x - high.astype(F32)).astype(BF16)
    return jnp.concatenate([high, low], axis=1)


def fold(x):
    half = x.shape[1] // 2
    return x[:, :half].astype(F32) + x[:, half:].astype(F32)


def dot(*pairs):
    parts = [jnp.dot(a, b, preferred_element_type=F32) for a, b in pairs]
    return fold(functools.reduce(jnp.add, parts))


def row_parity():
    return lax.rem(lax.axis_index("gx"), 2)


def col_parity():
    return lax.rem(lax.axis_index("gy"), 2)


def place(rho, rows):
    parity = row_parity()
    return rho + parity * (rows - 1 - 2 * rho)


def spot(rho, q):
    return (rho + 1) * WIDE + q + 1


def swap_far(rows, cols, hop):
    pairs = []
    for a in range(rows):
        for b in range(cols):
            partner = a - 1 if a % 2 == 0 else a + 1
            if 0 <= partner < rows:
                pairs.append((a * cols + b, partner * cols + b))
            elif hop:
                pairs.append((a * cols + b, a * cols + (b ^ hop)))
    return pairs


def swap_near(rows, cols):
    return [(a * cols + b, (a ^ 1) * cols + b) for a in range(rows) for b in range(cols)]


def swap_even(rows, cols):
    return [(a * cols + b, a * cols + (b ^ 1)) for a in range(rows) for b in range(cols)]


def swap_odd(rows, cols):
    pairs = []
    for a in range(rows):
        for b in range(cols):
            partner = b - 1 if b % 2 == 0 else b + 1
            if 0 <= partner < cols:
                pairs.append((a * cols + b, a * cols + partner))
            else:
                pairs.append((a * cols + b, (a ^ 1) * cols + b))
    return pairs


def far_is_inside():
    gx = lax.axis_index("gx")
    return jnp.where(row_parity() == 0, gx > 0, gx < lax.axis_size("gx") - 1)


def odd_is_inside():
    gy = lax.axis_index("gy")
    return jnp.where(col_parity() == 0, gy > 0, gy < lax.axis_size("gy") - 1)


def write_sides(grid, even_halo, odd_halo, rows):
    parity = col_parity()
    even_col = jnp.where(parity == 0, BLOCK_Y, -1)
    odd_col = BLOCK_Y - 1 - even_col
    inside = odd_is_inside()
    for rho in range(rows):
        grid[spot(rho, even_col)] = split(even_halo[rho])
        grid[spot(rho, odd_col)] = split(jnp.where(inside, odd_halo[rho], 0.0))


def read_sides(grid, even_send, odd_send, rows):
    parity = col_parity()
    even_col = jnp.where(parity == 0, BLOCK_Y - 1, 0)
    odd_col = BLOCK_Y - 1 - even_col
    for rho in range(rows):
        even_send[rho] = fold(grid[spot(rho, even_col)])
        odd_send[rho] = fold(grid[spot(rho, odd_col)])


def write_row(grid, halo, rho, cols, inside=None):
    for n, q in enumerate(cols):
        value = halo[n]
        if inside is not None:
            value = jnp.where(inside, value, 0.0)
        grid[spot(rho, q)] = split(value)


def read_row(grid, send, rho, cols):
    for n, q in enumerate(cols):
        send[n] = fold(grid[spot(rho, q)])


def over_rows(first, last, body):
    def step(rho, carry):
        body(rho)
        return carry

    lax.fori_loop(first, last, step, 0)


def with_zeros(own, after):
    none = jnp.zeros(own.shape, BF16)
    return jnp.concatenate([own, none] if after else [none, own], axis=0)


def smoothed(blocks, cell, side):
    species = side.shape[0]
    return dot((blocks[cell, :, -2 * species :], with_zeros(split(side), False)))


def fine_cell(rho, q):
    return place(rho, BLOCK_X) * BLOCK_Y + q


def fine_apply(rho, q, blocks, grid):
    cell = fine_cell(rho, q)
    species = blocks.shape[1]
    here = spot(rho, q)
    step = WIDE * (1 - 2 * row_parity())
    near = jnp.concatenate([grid[here - step], grid[here + step], grid[here - 1], grid[here + 1]], axis=0)
    return dot(
        (blocks[cell, :, : 4 * species], near), (blocks[cell, :, 4 * species :], with_zeros(grid[here], True))
    )


def fine_second(rho, cols, blocks, grid, side, change, iterate, first, far=None):
    fine_cells([(rho, q, first + q) for q in cols], blocks, grid, side, change, iterate, far)


def fine_cells(cells, blocks, grid, side, change, iterate, far=None):
    for rho, q, _ in cells:
        cell = fine_cell(rho, q)
        side[cell] = side[cell] - fine_apply(rho, q, blocks, grid)
    for m, (rho, q, n) in enumerate(cells):
        cell = fine_cell(rho, q)
        here = spot(rho, q)
        step = smoothed(blocks, cell, side[cell])
        change[here] = split(step)
        iterate[n] = fold(grid[here]) + step
        if far is not None:
            far[m] = step


def fine_left(rho, q, blocks, side, change):
    return side[fine_cell(rho, q)] - fine_apply(rho, q, blocks, change)


def start_kernel(right, inverse, blocks, grid, side, far_m, far_n, inverse_here, sems):
    species = inverse.shape[0]
    part = species // 2
    loads = [
        pltpu.make_async_copy(inverse.at[pl.ds(n * part, part)], inverse_here.at[pl.ds(n * part, part)], sems.at[n])
        for n in range(2)
    ]
    for rho in range(BLOCK_X):
        row = pl.ds(fine_cell(rho, 0), BLOCK_Y)
        loads.append(pltpu.make_async_copy(right.at[row], side.at[row], sems.at[2 + rho]))
    for load in loads:
        load.start()
    for n in range(2):
        loads[n].wait()
        some = inverse_here[n * part : (n + 1) * part]
        both = jnp.concatenate([jnp.zeros(some.shape, BF16), some], axis=1)
        blocks[:, n * part : (n + 1) * part, 4 * species :] = jnp.transpose(both, (2, 0, 1))
    loads[2].wait()
    for cols, send in ((MIDDLE, far_m), (ENDS, far_n)):
        for n, q in enumerate(cols):
            cell = fine_cell(0, q)
            first = smoothed(blocks, cell, side[cell])
            grid[spot(0, q)] = split(first)
            send[n] = first
    for load in loads[3:]:
        load.wait()


def first_kernel(side, blocks, grid_in, grid, near, even, odd):
    def row(rho, near=None):
        for q in range(BLOCK_Y):
            cell = fine_cell(rho, q)
            first = smoothed(blocks, cell, side[cell])
            grid[spot(rho, q)] = split(first)
            if near is not None:
                near[q] = first

    over_rows(1, BLOCK_X - 1, row)
    row(BLOCK_X - 1, near)
    read_sides(grid, even, odd, BLOCK_X)


def fine_blocks_kernel(coupling, diagonal, inverse, blocks_in, near_in, blocks, near):
    species = coupling.shape[0]
    part = species // 2
    for first in range(0, species, part):
        rows = slice(first, first + part)
        blocks[:, rows, : 4 * species] = jnp.transpose(coupling[rows], (2, 0, 1))
        both = jnp.concatenate([diagonal[rows], inverse[rows]], axis=1)
        blocks[:, rows, 4 * species :] = jnp.transpose(both, (2, 0, 1))


def fine_inner_kernel(blocks, grid, side_in, side, change, held):
    for rho in range(1, BLOCK_X - 1):
        fine_second(rho, INSIDE, blocks, grid, side, change, held, (rho - 1) * BLOCK_Y)


def fine_middle_kernel(cols, blocks, far_h, grid_in, side_in, change_in, grid, side, change, iterate, far):
    write_row(grid, far_h, -1, cols, far_is_inside())
    fine_second(0, cols, blocks, grid, side, change, iterate, 0, far)


def fine_last_kernel(
    blocks, near_h, even_h, odd_h, grid_in, side_in, change_in, grid, side, change, last, near
):
    write_row(grid, near_h, BLOCK_X, range(BLOCK_Y))
    write_sides(grid, even_h, odd_h, BLOCK_X)
    fine_second(BLOCK_X - 1, range(BLOCK_Y), blocks, grid, side, change, last, 0, near)


def fine_ends_kernel(
    cols,
    blocks,
    far_h,
    grid_in,
    side_in,
    change_in,
    iterate_in,
    held_in,
    grid,
    side,
    change,
    iterate,
    held,
    far,
    even,
    odd,
):
    write_row(grid, far_h, -1, cols, far_is_inside())
    fine_second(0, cols, blocks, grid, side, change, iterate, 0, far)
    others = [(rho, q, (rho - 1) * BLOCK_Y + q) for rho in range(1, BLOCK_X - 1) for q in SIDES]
    fine_cells(others, blocks, grid, side, change, held)
    read_sides(change, even, odd, BLOCK_X)


def left_pair(rho, cols, blocks, side, change, coarse_side, own_blocks, coarse_grid, far=None, shift=0):
    for q in cols:
        upper = fine_left(2 * rho, q, blocks, side, change)
        coarse_side[rho * BLOCK_Y + q] = upper + fine_left(2 * rho + 1, q, blocks, side, change)
    for n, q in enumerate(cols):
        cell = place(rho, COARSE_X) * BLOCK_Y + q
        first = smoothed(own_blocks, cell, coarse_side[rho * BLOCK_Y + q])
        coarse_grid[spot(rho, q)] = split(first)
        if far is not None:
            far[n + shift] = first


def left_middle_kernel(cols, blocks, side, own_blocks, far_h, change_in, change, coarse_side, coarse_grid, far):
    write_row(change, far_h, -1, cols, far_is_inside())
    left_pair(0, cols, blocks, side, change, coarse_side, own_blocks, coarse_grid, far)


def left_halo_kernel(near_h, even_h, odd_h, change_in, change):
    write_row(change, near_h, BLOCK_X, range(BLOCK_Y))
    write_sides(change, even_h, odd_h, BLOCK_X)


def left_ends_kernel(
    cols,
    blocks,
    side,
    own_blocks,
    far_h,
    change_in,
    coarse_in,
    grid_in,
    change,
    coarse_side,
    coarse_grid,
    far,
    even,
    odd,
):
    write_row(change, far_h, -1, cols, far_is_inside())
    left_pair(0, cols, blocks, side, change, coarse_side, own_blocks, coarse_grid, far)
    for rho in range(1, COARSE_X):
        left_pair(rho, SIDES, blocks, side, change, coarse_side, own_blocks, coarse_grid)
    read_sides(coarse_grid, even, odd, COARSE_X)


def left_inner_kernel(blocks, side, own_blocks, change, coarse_in, grid_in, coarse_side, coarse_grid, near):
    for rho in range(1, COARSE_X):
        last = near if rho == COARSE_X - 1 else None
        left_pair(rho, INSIDE, blocks, side, change, coarse_side, own_blocks, coarse_grid, last, INSIDE[0])
    for q in SIDES:
        near[q] = fold(coarse_grid[spot(COARSE_X - 1, q)])


def near_blocks_kernel(coupling, first_row, held, last_row, blocks, out, sems):
    species = coupling.shape[1]
    step, count = pl.program_id(0), coupling.shape[0]
    copies = []
    for rho in range(BLOCK_X):
        source = first_row if rho == 0 else last_row
        if 0 < rho < BLOCK_X - 1:
            source = held.at[pl.ds((rho - 1) * BLOCK_Y, BLOCK_Y)]
        target = out.at[pl.ds(fine_cell(rho, 0), BLOCK_Y)]
        copies.append(pltpu.make_async_copy(source, target, sems.at[rho]))

    @pl.when(step == 0)
    def _():
        for copy in copies:
            copy.start()

    for n in range(count):
        blocks[step * count + n] = coupling[n].reshape(species, 8 * species)

    @pl.when(step == pl.num_programs(0) - 1)
    def _():
        for copy in copies:
            copy.wait()


def coarse_apply(rho, q, places, blocks, own_blocks, grid):
    cell = place(rho, COARSE_X) * BLOCK_Y + q
    near = jnp.concatenate([grid[places[k, cell]] for k in range(8)], axis=0)
    return dot((blocks[cell], near), (own_blocks[cell], with_zeros(grid[spot(rho, q)], True)))


def coarse_second(rho, cols, places, blocks, own_blocks, grid, side, change, iterate, far=None, shift=0):
    for q in cols:
        here = rho * BLOCK_Y + q
        side[here] = side[here] - coarse_apply(rho, q, places, blocks, own_blocks, grid)
    for m, q in enumerate(cols):
        here = spot(rho, q)
        cell = place(rho, COARSE_X) * BLOCK_Y + q
        step = smoothed(own_blocks, cell, side[rho * BLOCK_Y + q])
        change[here] = split(step)
        iterate[cell] = fold(grid[here]) + step
        if far is not None:
            far[m + shift] = step


def pack_kernel(even_h, odd_h, grid_in, grid, far, near):
    write_sides(grid, even_h, odd_h, COARSE_X)
    read_row(grid, far, 0, BESIDE)
    read_row(grid, near, COARSE_X - 1, BESIDE)


def row_out(source, out, rho, sem):
    some = pl.ds(place(rho, COARSE_X) * BLOCK_Y, BLOCK_Y)
    return pltpu.make_async_copy(source.at[some], out.at[some], sem)


def coarse_inner_kernel(
    places, blocks, own_blocks, grid, side_in, change_in, iterate_in, side, change, iterate, near, out, sem
):
    leave = row_out(iterate, out, 0, sem)
    leave.start()
    for rho in range(1, COARSE_X):
        last = near if rho == COARSE_X - 1 else None
        coarse_second(rho, INSIDE, places, blocks, own_blocks, grid, side, change, iterate, last, INSIDE[0])
    for q in SIDES:
        near[q] = fold(change[spot(COARSE_X - 1, q)])
    leave.wait()


def coarse_halo_kernel(near_h, beside_h, grid_in, grid):
    write_row(grid, near_h, COARSE_X, range(BLOCK_Y))
    write_row(grid, beside_h, COARSE_X, BESIDE)


def coarse_middle_kernel(
    came, cols, places, blocks, own_blocks, far_h, grid_in, side_in, grid, side, change, iterate, far
):
    write_row(grid, far_h, -1, came)
    coarse_second(0, cols, places, blocks, own_blocks, grid, side, change, iterate, far)


class InTwo:
    def __init__(self, low, high):
        self.low, self.high = low, high

    def __setitem__(self, n, value):
        count = self.low.shape[0]
        if n < count:
            self.low[n] = value
        else:
            self.high[n - count] = value


def coarse_ends_kernel(
    came,
    cols,
    places,
    blocks,
    own_blocks,
    far_h,
    corners_h,
    grid_in,
    side_in,
    change_in,
    iterate_in,
    grid,
    side,
    change,
    iterate,
    low,
    high,
    even,
    odd,
):
    far = InTwo(low, high)
    write_row(grid, far_h, -1, came)
    write_row(grid, corners_h, -1, BESIDE)
    coarse_second(0, cols, places, blocks, own_blocks, grid, side, change, iterate, far)
    for rho in range(1, COARSE_X):
        coarse_second(rho, SIDES, places, blocks, own_blocks, grid, side, change, iterate)
    read_sides(change, even, odd, COARSE_X)


def last_pairs(rho, pairs, places, blocks, own_blocks, side, change, below):
    first = place(rho, COARSE_X) * (BLOCK_Y // 2)
    for pair in pairs:
        q = 2 * pair
        total = side[rho * BLOCK_Y + q] + side[rho * BLOCK_Y + q + 1]
        total = total - coarse_apply(rho, q, places, blocks, own_blocks, change)
        total = total - coarse_apply(rho, q + 1, places, blocks, own_blocks, change)
        below[first + pair] = total


def last_middle_kernel(came, pairs, places, blocks, own_blocks, side, far_h, change_in, change, below):
    write_row(change, far_h, -1, came)
    last_pairs(0, pairs, places, blocks, own_blocks, side, change, below)


def last_inner_kernel(
    pairs, places, blocks, own_blocks, side, near_h, iterate, change_in, below_in, out_in, change, below, out, sems
):
    leave = [row_out(iterate, out, rho, sems.at[rho]) for rho in range(1, COARSE_X)]
    for copy in leave:
        copy.start()
    write_row(change, near_h, COARSE_X, range(BLOCK_Y))
    for rho in range(1, COARSE_X):
        last_pairs(rho, pairs, places, blocks, own_blocks, side, change, below)
    for copy in leave:
        copy.wait()


def last_sides_kernel(todo, places, blocks, own_blocks, side, beside_h, change_in, below_in, change, below):
    write_row(change, beside_h, COARSE_X, BESIDE)
    for rho in range(1, COARSE_X):
        last_pairs(rho, todo, places, blocks, own_blocks, side, change, below)


def last_low_kernel(
    came, todo, places, blocks, own_blocks, side, far_h, corners_h, change_in, below_in, change, below
):
    write_row(change, far_h, -1, came)
    write_row(change, corners_h, -1, BESIDE)
    last_pairs(0, todo, places, blocks, own_blocks, side, change, below)


def last_high_kernel(came, todo, places, blocks, own_blocks, side, far_h, change_in, below, change, out, made, sems):
    half = BLOCK_Y // 2
    copies = []

    def send(source, rho, first, count):
        some = pl.ds(place(rho, COARSE_X) * half + first, count)
        copies.append(pltpu.make_async_copy(source.at[some], out.at[some], sems.at[len(copies)]))
        copies[-1].start()

    for rho in range(1, COARSE_X):
        send(below, rho, 0, half)
    send(below, 0, 0, todo[0])
    write_row(change, far_h, -1, came)
    last_pairs(0, todo, places, blocks, own_blocks, side, change, made)
    send(made, 0, todo[0], len(todo))
    for copy in copies:
        copy.wait()


IN_VMEM = pl.BlockSpec(memory_space=pltpu.VMEM)
IN_HBM = pl.BlockSpec(memory_space=pltpu.HBM)
LONG = 10**11


def run(name, kernel, outs, args, aliases=(), smem=(), hbm=(), hbm_outs=(), smem_outs=(), scratch=(), after=(), cost=1, room=2):
    count = len(args)
    args = list(args) + list(after)
    spaces = [pltpu.SMEM if n in smem else pltpu.HBM if n in hbm else pltpu.VMEM for n in range(len(args))]
    out_spaces = [
        pltpu.SMEM if n in smem_outs else pltpu.HBM if n in hbm_outs else pltpu.VMEM for n in range(len(outs))
    ]

    def body(*refs):
        kernel(*refs[:count], *refs[len(args) :])

    called = pl.pallas_call(
        body,
        out_shape=tuple(space(shape, dtype) for space, (shape, dtype) in zip(out_spaces, outs)),
        in_specs=[pl.BlockSpec(memory_space=space) for space in spaces],
        out_specs=tuple(pl.BlockSpec(memory_space=space) for space in out_spaces),
        scratch_shapes=list(scratch),
        input_output_aliases=dict(aliases),
        compiler_params=pltpu.CompilerParams(vmem_limit_bytes=room * 2**20),
        cost_estimate=pl.CostEstimate(flops=cost, bytes_accessed=1, transcendentals=0),
        name=name,
    )
    return called(*(pltpu.with_memory_space_constraint(x, space) for x, space in zip(args, spaces)))


def near_blocks_call(coupling, first_row, held, last_row, count):
    cells, species = coupling.shape[:2]
    part = cells // 8
    here = [pltpu.with_memory_space_constraint(x, pltpu.VMEM) for x in (first_row, held, last_row)]
    return pl.pallas_call(
        near_blocks_kernel,
        grid=(cells // part,),
        out_shape=(
            pltpu.VMEM((cells, species, 8 * species), BF16),
            pltpu.HBM((count,) + first_row.shape[1:], F32),
        ),
        in_specs=[
            pl.BlockSpec((part,) + coupling.shape[1:], lambda n: (n, 0, 0, 0)),
            IN_VMEM,
            IN_VMEM,
            IN_VMEM,
        ],
        out_specs=(IN_VMEM, IN_HBM),
        scratch_shapes=[pltpu.SemaphoreType.DMA((BLOCK_X,))],
        compiler_params=pltpu.CompilerParams(vmem_limit_bytes=5 * 2**20),
        cost_estimate=pl.CostEstimate(flops=1, bytes_accessed=1, transcendentals=0),
        name="near_blocks",
    )(coupling, *here)


def own_blocks_kernel(across, diagonal, inverse, pattern, blocks, places, made, sem):
    number = pattern[...]
    per_block = COARSE_X * BLOCK_Y
    owner = lax.div(number, per_block)
    inside = lax.rem(number, per_block)
    row = lax.div(owner, across) * COARSE_X + lax.div(inside, BLOCK_Y) - lax.axis_index("gx") * COARSE_X
    col = lax.rem(owner, across) * BLOCK_Y + lax.rem(inside, BLOCK_Y) - lax.axis_index("gy") * BLOCK_Y
    rho = jnp.where(row_parity() == 0, row, COARSE_X - 1 - row)
    made[...] = (rho + 1) * WIDE + col + 1
    copy = pltpu.make_async_copy(made, places, sem)
    copy.start()
    for cell in range(diagonal.shape[0]):
        blocks[cell] = jnp.concatenate([diagonal[cell], inverse[cell]], axis=1)
    copy.wait()


def on_device(
    right_side,
    fine_coupling,
    fine_diagonal,
    fine_inverse,
    coarse_coupling,
    coarse_diagonal,
    coarse_inverse,
    coarse_pattern,
):
    cells, species, vectors = right_side.shape
    coarse_cells = coarse_coupling.shape[0]
    rows, cols = lax.axis_size("gx"), lax.axis_size("gy")
    far_pairs, near_pairs = swap_far(rows, cols, 2 if cols % 4 == 0 else 1), swap_near(rows, cols)
    corner_pairs = swap_far(rows, cols, 1)
    even_pairs, odd_pairs = swap_even(rows, cols), swap_odd(rows, cols)

    def far(x):
        return lax.ppermute(x, BOTH, far_pairs)

    def near(x):
        return lax.ppermute(x, BOTH, near_pairs)

    def even(x):
        return lax.ppermute(x, BOTH, even_pairs)

    def odd(x):
        return lax.ppermute(x, BOTH, odd_pairs)

    def field(count):
        return ((count, species, vectors), F32)

    def padded(count):
        return (((count + 2) * WIDE, species, 2 * vectors), BF16)

    fine_blocks = ((cells, species, 6 * species), BF16)
    coupling = jnp.transpose(fine_coupling, (1, 2, 3, 0)).reshape(species, 4 * species, cells)
    diagonal = jnp.transpose(fine_diagonal, (1, 2, 0))
    inverse = jnp.transpose(fine_inverse, (1, 2, 0))
    pattern = coarse_pattern.T
    middle, ends = len(MIDDLE), len(ENDS)

    blocks, grid, side, far_m, far_n = run(
        "start",
        start_kernel,
        [fine_blocks, padded(BLOCK_X), field(cells), field(middle), field(ends)],
        [right_side, inverse],
        hbm=(0, 1),
        scratch=[pltpu.VMEM(inverse.shape, BF16), pltpu.SemaphoreType.DMA((2 + BLOCK_X,))],
        room=6,
    )
    far_m, far_n = lax.ppermute(far_m, BOTH, swap_far(rows, cols, 0)), far(far_n)
    grid, near_s, even_s, odd_s = run(
        "first",
        first_kernel,
        [padded(BLOCK_X), field(BLOCK_Y), field(BLOCK_X), field(BLOCK_X)],
        [side, blocks, grid],
        [(2, 0)],
    )
    even_h, odd_h = even(even_s), odd(odd_s)
    blocks, near_s = run(
        "fine_blocks",
        fine_blocks_kernel,
        [fine_blocks, field(BLOCK_Y)],
        [coupling, diagonal, inverse, blocks, near_s],
        [(3, 0), (4, 1)],
        room=6,
    )
    near_h = near(near_s)
    state = [padded(BLOCK_X), field(cells), padded(BLOCK_X)]
    side, change, held = run(
        "fine_inner",
        fine_inner_kernel,
        state[1:] + [field((BLOCK_X - 2) * BLOCK_Y)],
        [blocks, grid, side],
        [(2, 0)],
    )
    grid, side, change, iterate, far_m = run(
        "fine_middle",
        functools.partial(fine_middle_kernel, MIDDLE),
        state + [field(BLOCK_Y), field(middle)],
        [blocks, far_m, grid, side, change],
        [(2, 0), (3, 1), (4, 2)],
        after=[even_h, odd_h],
        cost=LONG,
    )
    far_m = far(far_m)
    grid, side, change, last_row, near_s = run(
        "fine_last",
        fine_last_kernel,
        state + [field(BLOCK_Y), field(BLOCK_Y)],
        [blocks, near_h, even_h, odd_h, grid, side, change],
        [(4, 0), (5, 1), (6, 2)],
    )
    near_h = near(near_s)
    grid, side, change, iterate, held, far_n, even_s, odd_s = run(
        "fine_ends",
        functools.partial(fine_ends_kernel, ENDS),
        state
        + [field(BLOCK_Y), field((BLOCK_X - 2) * BLOCK_Y), field(ends), field(BLOCK_X), field(BLOCK_X)],
        [blocks, far_n, grid, side, change, iterate, held],
        [(2, 0), (3, 1), (4, 2), (5, 3), (6, 4)],
    )
    own_blocks, places = run(
        "own_blocks",
        functools.partial(own_blocks_kernel, cols),
        [((coarse_cells, species, 2 * species), BF16), (pattern.shape, jnp.int32)],
        [coarse_diagonal, coarse_inverse, pattern],
        smem_outs=(1,),
        scratch=[pltpu.VMEM(pattern.shape, jnp.int32), pltpu.SemaphoreType.DMA],
        after=[far_n],
    )
    near_blocks, fine_iterate = near_blocks_call(coarse_coupling, iterate, held, last_row, cells)
    far_n = far(far_n)
    even_h, odd_h = even(even_s), odd(odd_s)

    state = [padded(BLOCK_X), field(coarse_cells), padded(COARSE_X)]
    change, coarse_side, coarse_grid, far_m = run(
        "left_middle",
        functools.partial(left_middle_kernel, MIDDLE),
        state + [field(middle)],
        [blocks, side, own_blocks, far_m, change],
        [(4, 0)],
        after=[even_h, odd_h, near_blocks],
        cost=LONG,
    )
    far_m = far(far_m)
    (change,) = run(
        "left_halo", left_halo_kernel, [padded(BLOCK_X)], [near_h, even_h, odd_h, change], [(3, 0)]
    )
    change, coarse_side, coarse_grid, far_n, even_s, odd_s = run(
        "left_ends",
        functools.partial(left_ends_kernel, ENDS),
        state + [field(ends), field(COARSE_X), field(COARSE_X)],
        [blocks, side, own_blocks, far_n, change, coarse_side, coarse_grid],
        [(4, 0), (5, 1), (6, 2)],
        cost=LONG,
    )
    coarse_side, coarse_grid, near_s = run(
        "left_inner",
        left_inner_kernel,
        state[1:] + [field(BLOCK_Y)],
        [blocks, side, own_blocks, change, coarse_side, coarse_grid],
        [(4, 0), (5, 1)],
    )
    far_n = far(far_n)
    even_h, odd_h = even(even_s), odd(odd_s)
    near_h = near(near_s)
    coarse_grid, corners, beside = run(
        "pack_first",
        pack_kernel,
        [padded(COARSE_X), field(2), field(2)],
        [even_h, odd_h, coarse_grid],
        [(2, 0)],
    )
    corners, beside = lax.ppermute(corners, BOTH, corner_pairs), near(beside)

    state = [padded(COARSE_X), field(coarse_cells), padded(COARSE_X), field(coarse_cells)]
    inner = MIDDLE[1:-1]
    outer = tuple(q for q in range(BLOCK_Y) if q not in inner)
    coarse_grid, coarse_side, coarse_change, iterate, far_m = run(
        "coarse_middle",
        functools.partial(coarse_middle_kernel, MIDDLE, inner),
        state + [field(len(inner))],
        [places, near_blocks, own_blocks, far_m, coarse_grid, coarse_side],
        [(4, 0), (5, 1)],
        smem=(0,),
        cost=LONG,
    )
    far_m = far(far_m)
    (coarse_grid,) = run(
        "coarse_halo", coarse_halo_kernel, [padded(COARSE_X)], [near_h, beside, coarse_grid], [(2, 0)]
    )
    low, high = (tuple(q for q in outer if (q < inner[0]) == first) for first in (True, False))
    coarse_grid, coarse_side, coarse_change, iterate, far_low, far_high, even_s, odd_s = run(
        "coarse_ends",
        functools.partial(coarse_ends_kernel, ENDS, outer),
        state + [field(len(low)), field(len(high)), field(COARSE_X), field(COARSE_X)],
        [places, near_blocks, own_blocks, far_n, corners, coarse_grid, coarse_side, coarse_change, iterate],
        [(5, 0), (6, 1), (7, 2), (8, 3)],
        smem=(0,),
        cost=LONG,
    )
    coarse_side, coarse_change, iterate, near_s, coarse_iterate = run(
        "coarse_inner",
        coarse_inner_kernel,
        state[1:] + [field(BLOCK_Y), field(coarse_cells)],
        [places, near_blocks, own_blocks, coarse_grid, coarse_side, coarse_change, iterate],
        [(4, 0), (5, 1), (6, 2)],
        smem=(0,),
        hbm_outs=(4,),
        scratch=[pltpu.SemaphoreType.DMA],
    )
    far_low, far_high = far(far_low), far(far_high)
    even_h, odd_h = even(even_s), odd(odd_s)
    near_h = near(near_s)
    coarse_change, corners, beside = run(
        "pack_second",
        pack_kernel,
        [padded(COARSE_X), field(2), field(2)],
        [even_h, odd_h, coarse_change],
        [(2, 0)],
    )
    corners, beside = lax.ppermute(corners, BOTH, corner_pairs), near(beside)

    state = [padded(COARSE_X), field(coarse_cells // 2)]
    half = BLOCK_Y // 2
    core = tuple(q // 2 for q in inner[1:-1:2])
    pairs = tuple(range(1, half - 1))
    coarse_change, below = run(
        "last_middle",
        functools.partial(last_middle_kernel, inner, core),
        state,
        [places, near_blocks, own_blocks, coarse_side, far_m, coarse_change],
        [(5, 0)],
        smem=(0,),
        cost=LONG,
    )
    coarse_change, below, coarse_iterate = run(
        "last_inner",
        functools.partial(last_inner_kernel, pairs),
        state + [field(coarse_cells)],
        [places, near_blocks, own_blocks, coarse_side, near_h, iterate, coarse_change, below, coarse_iterate],
        [(6, 0), (7, 1), (8, 2)],
        smem=(0,),
        hbm=(8,),
        hbm_outs=(2,),
        scratch=[pltpu.SemaphoreType.DMA((COARSE_X,))],
    )
    coarse_change, below = run(
        "last_sides",
        functools.partial(last_sides_kernel, (0, half - 1)),
        state,
        [places, near_blocks, own_blocks, coarse_side, beside, coarse_change, below],
        [(5, 0), (6, 1)],
        smem=(0,),
    )
    coarse_change, below = run(
        "last_low",
        functools.partial(last_low_kernel, low, tuple(range(core[0]))),
        state,
        [places, near_blocks, own_blocks, coarse_side, far_low, corners, coarse_change, below],
        [(6, 0), (7, 1)],
        smem=(0,),
    )
    coarse_change, next_side = run(
        "last_high",
        functools.partial(last_high_kernel, high, tuple(range(core[-1] + 1, half))),
        state,
        [places, near_blocks, own_blocks, coarse_side, far_high, coarse_change, below],
        [(5, 0)],
        smem=(0,),
        hbm_outs=(1,),
        scratch=[pltpu.VMEM(state[1][0], F32), pltpu.SemaphoreType.DMA((COARSE_X + 1,))],
        room=3,
    )
    return (fine_iterate, coarse_iterate, next_side)


def solution(mesh):
    placed = (
        P(BOTH, None, None),
        P(BOTH, None, None, None),
        P(BOTH, None, None),
        P(BOTH, None, None),
        P(BOTH, None, None, None),
        P(BOTH, None, None),
        P(BOTH, None, None),
        P(BOTH, None),
    )
    return jax.shard_map(
        on_device,
        mesh=mesh,
        in_specs=placed,
        out_specs=(P(BOTH, None, None), P(BOTH, None, None), P(BOTH, None, None)),
        check_vma=False,
    )
```

```python
import functools

import jax
import jax.numpy as jnp
from jax import lax
from jax.experimental import pallas as pl
from jax.experimental.pallas import tpu as pltpu
from jax.sharding import PartitionSpec as P

BLOCK_X = 4
BLOCK_Y = 32

WIDE = BLOCK_Y + 2
COARSE_X = BLOCK_X // 2
EDGE = BLOCK_Y // 4
MIDDLE = tuple(range(EDGE, BLOCK_Y - EDGE))
ENDS = tuple(q for q in range(BLOCK_Y) if q not in MIDDLE)
SIDES = (0, BLOCK_Y - 1)
BESIDE = (-1, BLOCK_Y)
BORDER = (-1, 0, BLOCK_Y - 1, BLOCK_Y)
INSIDE = tuple(range(1, BLOCK_Y - 1))

F32 = jnp.float32
BF16 = jnp.bfloat16
BOTH = ("gx", "gy")


def split(x):
    high = x.astype(BF16)
    low = (x - high.astype(F32)).astype(BF16)
    return jnp.concatenate([high, low], axis=1)


def fold(x):
    half = x.shape[1] // 2
    return x[:, :half].astype(F32) + x[:, half:].astype(F32)


def dot(*pairs):
    parts = [jnp.dot(a, b, preferred_element_type=F32) for a, b in pairs]
    return fold(functools.reduce(jnp.add, parts))


def row_parity():
    return lax.rem(lax.axis_index("gx"), 2)


def col_parity():
    return lax.rem(lax.axis_index("gy"), 2)


def place(rho, rows):
    parity = row_parity()
    return rho + parity * (rows - 1 - 2 * rho)


def spot(rho, q):
    return (rho + 1) * WIDE + q + 1


def swap_far(rows, cols, hop):
    pairs = []
    for a in range(rows):
        for b in range(cols):
            partner = a - 1 if a % 2 == 0 else a + 1
            if 0 <= partner < rows:
                pairs.append((a * cols + b, partner * cols + b))
            elif hop:
                pairs.append((a * cols + b, a * cols + (b ^ hop)))
    return pairs


def swap_near(rows, cols):
    return [(a * cols + b, (a ^ 1) * cols + b) for a in range(rows) for b in range(cols)]


def swap_even(rows, cols):
    return [(a * cols + b, a * cols + (b ^ 1)) for a in range(rows) for b in range(cols)]


def swap_odd(rows, cols):
    pairs = []
    for a in range(rows):
        for b in range(cols):
            partner = b - 1 if b % 2 == 0 else b + 1
            if 0 <= partner < cols:
                pairs.append((a * cols + b, a * cols + partner))
            else:
                pairs.append((a * cols + b, (a ^ 1) * cols + b))
    return pairs


def far_is_inside():
    gx = lax.axis_index("gx")
    return jnp.where(row_parity() == 0, gx > 0, gx < lax.axis_size("gx") - 1)


def odd_is_inside():
    gy = lax.axis_index("gy")
    return jnp.where(col_parity() == 0, gy > 0, gy < lax.axis_size("gy") - 1)


def write_sides(grid, even_halo, odd_halo, rows):
    parity = col_parity()
    even_col = jnp.where(parity == 0, BLOCK_Y, -1)
    odd_col = BLOCK_Y - 1 - even_col
    inside = odd_is_inside()
    for rho in range(rows):
        grid[spot(rho, even_col)] = split(even_halo[rho])
        grid[spot(rho, odd_col)] = split(jnp.where(inside, odd_halo[rho], 0.0))


def read_sides(grid, even_send, odd_send, rows):
    parity = col_parity()
    even_col = jnp.where(parity == 0, BLOCK_Y - 1, 0)
    odd_col = BLOCK_Y - 1 - even_col
    for rho in range(rows):
        even_send[rho] = fold(grid[spot(rho, even_col)])
        odd_send[rho] = fold(grid[spot(rho, odd_col)])


def write_row(grid, halo, rho, cols, inside=None):
    for n, q in enumerate(cols):
        value = halo[n]
        if inside is not None:
            value = jnp.where(inside, value, 0.0)
        grid[spot(rho, q)] = split(value)


def read_row(grid, send, rho, cols):
    for n, q in enumerate(cols):
        send[n] = fold(grid[spot(rho, q)])


def over_rows(first, last, body):
    def step(rho, carry):
        body(rho)
        return carry

    lax.fori_loop(first, last, step, 0)


def with_zeros(own, after):
    none = jnp.zeros(own.shape, BF16)
    return jnp.concatenate([own, none] if after else [none, own], axis=0)


def smoothed(blocks, cell, side):
    species = side.shape[0]
    return dot((blocks[cell, :, -2 * species :], with_zeros(split(side), False)))


def fine_cell(rho, q):
    return place(rho, BLOCK_X) * BLOCK_Y + q


def fine_apply(rho, q, blocks, grid):
    cell = fine_cell(rho, q)
    species = blocks.shape[1]
    here = spot(rho, q)
    step = WIDE * (1 - 2 * row_parity())
    near = jnp.concatenate([grid[here - step], grid[here + step], grid[here - 1], grid[here + 1]], axis=0)
    return dot(
        (blocks[cell, :, : 4 * species], near), (blocks[cell, :, 4 * species :], with_zeros(grid[here], True))
    )


def fine_second(rho, cols, blocks, grid, side, change, iterate, first, far=None):
    fine_cells([(rho, q, first + q) for q in cols], blocks, grid, side, change, iterate, far)


def fine_cells(cells, blocks, grid, side, change, iterate, far=None):
    for rho, q, _ in cells:
        cell = fine_cell(rho, q)
        side[cell] = side[cell] - fine_apply(rho, q, blocks, grid)
    for m, (rho, q, n) in enumerate(cells):
        cell = fine_cell(rho, q)
        here = spot(rho, q)
        step = smoothed(blocks, cell, side[cell])
        change[here] = split(step)
        iterate[n] = fold(grid[here]) + step
        if far is not None:
            far[m] = step


def fine_left(rho, q, blocks, side, change):
    return side[fine_cell(rho, q)] - fine_apply(rho, q, blocks, change)


def start_kernel(right, inverse, blocks, grid, side, far_m, far_n, inverse_here, sems):
    species = inverse.shape[0]
    part = species // 2
    loads = [
        pltpu.make_async_copy(inverse.at[pl.ds(n * part, part)], inverse_here.at[pl.ds(n * part, part)], sems.at[n])
        for n in range(2)
    ]
    for rho in range(BLOCK_X):
        row = pl.ds(fine_cell(rho, 0), BLOCK_Y)
        loads.append(pltpu.make_async_copy(right.at[row], side.at[row], sems.at[2 + rho]))
    for load in loads:
        load.start()
    for n in range(2):
        loads[n].wait()
        some = inverse_here[n * part : (n + 1) * part]
        both = jnp.concatenate([jnp.zeros(some.shape, BF16), some], axis=1)
        blocks[:, n * part : (n + 1) * part, 4 * species :] = jnp.transpose(both, (2, 0, 1))
    loads[2].wait()
    for cols, send in ((MIDDLE, far_m), (ENDS, far_n)):
        for n, q in enumerate(cols):
            cell = fine_cell(0, q)
            first = smoothed(blocks, cell, side[cell])
            grid[spot(0, q)] = split(first)
            send[n] = first
    for load in loads[3:]:
        load.wait()


def first_kernel(side, blocks, grid_in, grid, near, even, odd):
    def row(rho, near=None):
        for q in range(BLOCK_Y):
            cell = fine_cell(rho, q)
            first = smoothed(blocks, cell, side[cell])
            grid[spot(rho, q)] = split(first)
            if near is not None:
                near[q] = first

    over_rows(1, BLOCK_X - 1, row)
    row(BLOCK_X - 1, near)
    read_sides(grid, even, odd, BLOCK_X)


def fine_blocks_kernel(coupling, diagonal, inverse, blocks_in, blocks):
    species = coupling.shape[0]
    part = species // 2
    for first in range(0, species, part):
        rows = slice(first, first + part)
        blocks[:, rows, : 4 * species] = jnp.transpose(coupling[rows], (2, 0, 1))
        both = jnp.concatenate([diagonal[rows], inverse[rows]], axis=1)
        blocks[:, rows, 4 * species :] = jnp.transpose(both, (2, 0, 1))


def fine_inner_kernel(blocks, grid, side_in, side, change, held):
    for rho in range(1, BLOCK_X - 1):
        fine_second(rho, INSIDE, blocks, grid, side, change, held, (rho - 1) * BLOCK_Y)


def fine_middle_kernel(cols, blocks, far_h, grid_in, side_in, change_in, grid, side, change, iterate, far):
    write_row(grid, far_h, -1, cols, far_is_inside())
    fine_second(0, cols, blocks, grid, side, change, iterate, 0, far)


def fine_last_kernel(
    blocks, near_h, even_h, odd_h, grid_in, side_in, change_in, grid, side, change, last, near
):
    write_row(grid, near_h, BLOCK_X, range(BLOCK_Y))
    write_sides(grid, even_h, odd_h, BLOCK_X)
    fine_second(BLOCK_X - 1, range(BLOCK_Y), blocks, grid, side, change, last, 0, near)


def fine_ends_kernel(
    cols,
    blocks,
    far_h,
    grid_in,
    side_in,
    change_in,
    iterate_in,
    held_in,
    grid,
    side,
    change,
    iterate,
    held,
    far,
    even,
    odd,
):
    write_row(grid, far_h, -1, cols, far_is_inside())
    fine_second(0, cols, blocks, grid, side, change, iterate, 0, far)
    others = [(rho, q, (rho - 1) * BLOCK_Y + q) for rho in range(1, BLOCK_X - 1) for q in SIDES]
    fine_cells(others, blocks, grid, side, change, held)
    read_sides(change, even, odd, BLOCK_X)


def left_pair(rho, cols, blocks, side, change, coarse_side, own_blocks, coarse_grid, far=None, shift=0):
    for q in cols:
        upper = fine_left(2 * rho, q, blocks, side, change)
        coarse_side[rho * BLOCK_Y + q] = upper + fine_left(2 * rho + 1, q, blocks, side, change)
    for n, q in enumerate(cols):
        cell = place(rho, COARSE_X) * BLOCK_Y + q
        first = smoothed(own_blocks, cell, coarse_side[rho * BLOCK_Y + q])
        coarse_grid[spot(rho, q)] = split(first)
        if far is not None:
            far[n + shift] = first


def left_middle_kernel(cols, blocks, side, own_blocks, far_h, change_in, change, coarse_side, coarse_grid, far):
    write_row(change, far_h, -1, cols, far_is_inside())
    left_pair(0, cols, blocks, side, change, coarse_side, own_blocks, coarse_grid, far)


def left_halo_kernel(near_h, even_h, odd_h, change_in, change):
    write_row(change, near_h, BLOCK_X, range(BLOCK_Y))
    write_sides(change, even_h, odd_h, BLOCK_X)


def left_ends_kernel(
    cols,
    blocks,
    side,
    own_blocks,
    far_h,
    change_in,
    coarse_in,
    grid_in,
    change,
    coarse_side,
    coarse_grid,
    far,
    even,
    odd,
):
    write_row(change, far_h, -1, cols, far_is_inside())
    left_pair(0, cols, blocks, side, change, coarse_side, own_blocks, coarse_grid, far)
    for rho in range(1, COARSE_X):
        left_pair(rho, SIDES, blocks, side, change, coarse_side, own_blocks, coarse_grid)
    read_sides(coarse_grid, even, odd, COARSE_X)


def left_inner_kernel(blocks, side, own_blocks, change, coarse_in, grid_in, coarse_side, coarse_grid, near):
    for rho in range(1, COARSE_X):
        last = near if rho == COARSE_X - 1 else None
        left_pair(rho, INSIDE, blocks, side, change, coarse_side, own_blocks, coarse_grid, last)


def near_blocks_kernel(coupling, first_row, held, last_row, blocks, out, sems):
    species = coupling.shape[1]
    step, count = pl.program_id(0), coupling.shape[0]
    copies = []
    for rho in range(BLOCK_X):
        source = first_row if rho == 0 else last_row
        if 0 < rho < BLOCK_X - 1:
            source = held.at[pl.ds((rho - 1) * BLOCK_Y, BLOCK_Y)]
        target = out.at[pl.ds(fine_cell(rho, 0), BLOCK_Y)]
        copies.append(pltpu.make_async_copy(source, target, sems.at[rho]))

    @pl.when(step == 0)
    def _():
        for copy in copies:
            copy.start()

    for n in range(count):
        blocks[step * count + n] = coupling[n].reshape(species, 8 * species)

    @pl.when(step == pl.num_programs(0) - 1)
    def _():
        for copy in copies:
            copy.wait()


def coarse_apply(rho, q, places, blocks, own_blocks, grid):
    cell = place(rho, COARSE_X) * BLOCK_Y + q
    near = jnp.concatenate([grid[places[k, cell]] for k in range(8)], axis=0)
    return dot((blocks[cell], near), (own_blocks[cell], with_zeros(grid[spot(rho, q)], True)))


def coarse_second(rho, cols, places, blocks, own_blocks, grid, side, change, iterate, far=None, shift=0):
    for q in cols:
        here = rho * BLOCK_Y + q
        side[here] = side[here] - coarse_apply(rho, q, places, blocks, own_blocks, grid)
    for m, q in enumerate(cols):
        here = spot(rho, q)
        cell = place(rho, COARSE_X) * BLOCK_Y + q
        step = smoothed(own_blocks, cell, side[rho * BLOCK_Y + q])
        change[here] = split(step)
        iterate[cell] = fold(grid[here]) + step
        if far is not None:
            far[m + shift] = step


def pack_kernel(even_h, odd_h, grid_in, grid, far, near):
    write_sides(grid, even_h, odd_h, COARSE_X)
    read_row(grid, far, 0, BESIDE)
    read_row(grid, near, COARSE_X - 1, BORDER)


def coarse_inner_kernel(places, blocks, own_blocks, grid, side_in, change_in, iterate_in, side, change, iterate, near):
    for rho in range(1, COARSE_X):
        last = near if rho == COARSE_X - 1 else None
        coarse_second(rho, INSIDE, places, blocks, own_blocks, grid, side, change, iterate, last)


def coarse_halo_kernel(near_h, beside_h, grid_in, grid):
    write_row(grid, near_h, COARSE_X, INSIDE)
    write_row(grid, beside_h, COARSE_X, BORDER)


def coarse_middle_kernel(
    came, cols, places, blocks, own_blocks, far_h, grid_in, side_in, grid, side, change, iterate, far
):
    write_row(grid, far_h, -1, came)
    coarse_second(0, cols, places, blocks, own_blocks, grid, side, change, iterate, far)


class InTwo:
    def __init__(self, low, high):
        self.low, self.high = low, high

    def __setitem__(self, n, value):
        count = self.low.shape[0]
        if n < count:
            self.low[n] = value
        else:
            self.high[n - count] = value


def coarse_ends_kernel(
    came,
    cols,
    places,
    blocks,
    own_blocks,
    far_h,
    corners_h,
    grid_in,
    side_in,
    change_in,
    iterate_in,
    grid,
    side,
    change,
    iterate,
    low,
    high,
    even,
    odd,
):
    far = InTwo(low, high)
    write_row(grid, far_h, -1, came)
    write_row(grid, corners_h, -1, BESIDE)
    coarse_second(0, cols, places, blocks, own_blocks, grid, side, change, iterate, far)
    for rho in range(1, COARSE_X):
        coarse_second(rho, SIDES, places, blocks, own_blocks, grid, side, change, iterate)
    read_sides(change, even, odd, COARSE_X)


def last_pairs(rho, pairs, places, blocks, own_blocks, side, change, below):
    first = place(rho, COARSE_X) * (BLOCK_Y // 2)
    for pair in pairs:
        q = 2 * pair
        total = side[rho * BLOCK_Y + q] + side[rho * BLOCK_Y + q + 1]
        total = total - coarse_apply(rho, q, places, blocks, own_blocks, change)
        total = total - coarse_apply(rho, q + 1, places, blocks, own_blocks, change)
        below[first + pair] = total


def last_middle_kernel(came, pairs, places, blocks, own_blocks, side, far_h, change_in, below_in, change, below):
    write_row(change, far_h, -1, came)
    last_pairs(0, pairs, places, blocks, own_blocks, side, change, below)


def last_inner_kernel(
    pairs, places, blocks, own_blocks, side, near_h, iterate, change_in, change, below, out, sem
):
    leave = pltpu.make_async_copy(iterate, out, sem)
    leave.start()
    write_row(change, near_h, COARSE_X, INSIDE)
    for rho in range(1, COARSE_X):
        last_pairs(rho, pairs, places, blocks, own_blocks, side, change, below)
    leave.wait()


def last_sides_kernel(todo, places, blocks, own_blocks, side, beside_h, change_in, below_in, change, below):
    write_row(change, beside_h, COARSE_X, BORDER)
    for rho in range(1, COARSE_X):
        last_pairs(rho, todo, places, blocks, own_blocks, side, change, below)


def last_low_kernel(came, todo, places, blocks, own_blocks, side, far_h, change_in, below_in, change, below):
    write_row(change, far_h, -1, came)
    last_pairs(0, todo, places, blocks, own_blocks, side, change, below)


def last_high_kernel(
    came, todo, places, blocks, own_blocks, side, change_in, below, corners_h, far_h, change, out, made, sems
):
    half = BLOCK_Y // 2
    copies = []

    def send(source, rho, first, count):
        some = pl.ds(place(rho, COARSE_X) * half + first, count)
        copies.append(pltpu.make_async_copy(source.at[some], out.at[some], sems.at[len(copies)]))
        copies[-1].start()

    for rho in range(1, COARSE_X):
        send(below, rho, 0, half)
    send(below, 0, 1, todo[0] - 1)
    write_row(change, corners_h, -1, BESIDE)
    write_row(change, far_h, -1, came)
    last_pairs(0, (0,) + todo, places, blocks, own_blocks, side, change, made)
    send(made, 0, 0, 1)
    send(made, 0, todo[0], len(todo))
    for copy in copies:
        copy.wait()


IN_VMEM = pl.BlockSpec(memory_space=pltpu.VMEM)
IN_HBM = pl.BlockSpec(memory_space=pltpu.HBM)
LONG = 10**11


def run(name, kernel, outs, args, aliases=(), smem=(), hbm=(), hbm_outs=(), smem_outs=(), scratch=(), after=(), cost=1, room=2):
    count = len(args)
    args = list(args) + list(after)
    spaces = [pltpu.SMEM if n in smem else pltpu.HBM if n in hbm else pltpu.VMEM for n in range(len(args))]
    out_spaces = [
        pltpu.SMEM if n in smem_outs else pltpu.HBM if n in hbm_outs else pltpu.VMEM for n in range(len(outs))
    ]

    def body(*refs):
        kernel(*refs[:count], *refs[len(args) :])

    called = pl.pallas_call(
        body,
        out_shape=tuple(space(shape, dtype) for space, (shape, dtype) in zip(out_spaces, outs)),
        in_specs=[pl.BlockSpec(memory_space=space) for space in spaces],
        out_specs=tuple(pl.BlockSpec(memory_space=space) for space in out_spaces),
        scratch_shapes=list(scratch),
        input_output_aliases=dict(aliases),
        compiler_params=pltpu.CompilerParams(vmem_limit_bytes=room * 2**20),
        cost_estimate=pl.CostEstimate(flops=cost, bytes_accessed=1, transcendentals=0),
        name=name,
    )
    return called(*(pltpu.with_memory_space_constraint(x, space) for x, space in zip(args, spaces)))


def near_blocks_call(coupling, first_row, held, last_row, count):
    cells, species = coupling.shape[:2]
    part = cells // 8
    here = [pltpu.with_memory_space_constraint(x, pltpu.VMEM) for x in (first_row, held, last_row)]
    return pl.pallas_call(
        near_blocks_kernel,
        grid=(cells // part,),
        out_shape=(
            pltpu.VMEM((cells, species, 8 * species), BF16),
            pltpu.HBM((count,) + first_row.shape[1:], F32),
        ),
        in_specs=[
            pl.BlockSpec((part,) + coupling.shape[1:], lambda n: (n, 0, 0, 0)),
            IN_VMEM,
            IN_VMEM,
            IN_VMEM,
        ],
        out_specs=(IN_VMEM, IN_HBM),
        scratch_shapes=[pltpu.SemaphoreType.DMA((BLOCK_X,))],
        compiler_params=pltpu.CompilerParams(vmem_limit_bytes=5 * 2**20),
        cost_estimate=pl.CostEstimate(flops=1, bytes_accessed=1, transcendentals=0),
        name="near_blocks",
    )(coupling, *here)


def own_blocks_kernel(across, diagonal, inverse, pattern, blocks, places, made, sem):
    number = pattern[...]
    per_block = COARSE_X * BLOCK_Y
    owner = lax.div(number, per_block)
    inside = lax.rem(number, per_block)
    row = lax.div(owner, across) * COARSE_X + lax.div(inside, BLOCK_Y) - lax.axis_index("gx") * COARSE_X
    col = lax.rem(owner, across) * BLOCK_Y + lax.rem(inside, BLOCK_Y) - lax.axis_index("gy") * BLOCK_Y
    rho = jnp.where(row_parity() == 0, row, COARSE_X - 1 - row)
    made[...] = (rho + 1) * WIDE + col + 1
    copy = pltpu.make_async_copy(made, places, sem)
    copy.start()
    for cell in range(diagonal.shape[0]):
        blocks[cell] = jnp.concatenate([diagonal[cell], inverse[cell]], axis=1)
    copy.wait()


def on_device(
    right_side,
    fine_coupling,
    fine_diagonal,
    fine_inverse,
    coarse_coupling,
    coarse_diagonal,
    coarse_inverse,
    coarse_pattern,
):
    cells, species, vectors = right_side.shape
    coarse_cells = coarse_coupling.shape[0]
    rows, cols = lax.axis_size("gx"), lax.axis_size("gy")
    far_pairs, near_pairs = swap_far(rows, cols, 2 if cols % 4 == 0 else 1), swap_near(rows, cols)
    corner_pairs = swap_far(rows, cols, 1)
    even_pairs, odd_pairs = swap_even(rows, cols), swap_odd(rows, cols)

    def far(x):
        return lax.ppermute(x, BOTH, far_pairs)

    def near(x):
        return lax.ppermute(x, BOTH, near_pairs)

    def even(x):
        return lax.ppermute(x, BOTH, even_pairs)

    def odd(x):
        return lax.ppermute(x, BOTH, odd_pairs)

    def field(count):
        return ((count, species, vectors), F32)

    def padded(count):
        return (((count + 2) * WIDE, species, 2 * vectors), BF16)

    fine_blocks = ((cells, species, 6 * species), BF16)
    coupling = jnp.transpose(fine_coupling, (1, 2, 3, 0)).reshape(species, 4 * species, cells)
    diagonal = jnp.transpose(fine_diagonal, (1, 2, 0))
    inverse = jnp.transpose(fine_inverse, (1, 2, 0))
    pattern = coarse_pattern.T
    middle, ends = len(MIDDLE), len(ENDS)

    blocks, grid, side, far_m, far_n = run(
        "start",
        start_kernel,
        [fine_blocks, padded(BLOCK_X), field(cells), field(middle), field(ends)],
        [right_side, inverse],
        hbm=(0, 1),
        scratch=[pltpu.VMEM(inverse.shape, BF16), pltpu.SemaphoreType.DMA((2 + BLOCK_X,))],
        room=6,
    )
    far_m, far_n = lax.ppermute(far_m, BOTH, swap_far(rows, cols, 0)), far(far_n)
    grid, near_s, even_s, odd_s = run(
        "first",
        first_kernel,
        [padded(BLOCK_X), field(BLOCK_Y), field(BLOCK_X), field(BLOCK_X)],
        [side, blocks, grid],
        [(2, 0)],
    )
    near_h, even_h, odd_h = near(near_s), even(even_s), odd(odd_s)
    (blocks,) = run(
        "fine_blocks",
        fine_blocks_kernel,
        [fine_blocks],
        [coupling, diagonal, inverse, blocks],
        [(3, 0)],
        after=[near_s],
        room=6,
    )
    state = [padded(BLOCK_X), field(cells), padded(BLOCK_X)]
    side, change, held = run(
        "fine_inner",
        fine_inner_kernel,
        state[1:] + [field((BLOCK_X - 2) * BLOCK_Y)],
        [blocks, grid, side],
        [(2, 0)],
    )
    grid, side, change, iterate, far_m = run(
        "fine_middle",
        functools.partial(fine_middle_kernel, MIDDLE),
        state + [field(BLOCK_Y), field(middle)],
        [blocks, far_m, grid, side, change],
        [(2, 0), (3, 1), (4, 2)],
        after=[even_h, odd_h],
        cost=LONG,
    )
    far_m = far(far_m)
    grid, side, change, last_row, near_s = run(
        "fine_last",
        fine_last_kernel,
        state + [field(BLOCK_Y), field(BLOCK_Y)],
        [blocks, near_h, even_h, odd_h, grid, side, change],
        [(4, 0), (5, 1), (6, 2)],
    )
    near_h = near(near_s)
    grid, side, change, iterate, held, far_n, even_s, odd_s = run(
        "fine_ends",
        functools.partial(fine_ends_kernel, ENDS),
        state
        + [field(BLOCK_Y), field((BLOCK_X - 2) * BLOCK_Y), field(ends), field(BLOCK_X), field(BLOCK_X)],
        [blocks, far_n, grid, side, change, iterate, held],
        [(2, 0), (3, 1), (4, 2), (5, 3), (6, 4)],
    )
    own_blocks, places = run(
        "own_blocks",
        functools.partial(own_blocks_kernel, cols),
        [((coarse_cells, species, 2 * species), BF16), (pattern.shape, jnp.int32)],
        [coarse_diagonal, coarse_inverse, pattern],
        smem_outs=(1,),
        scratch=[pltpu.VMEM(pattern.shape, jnp.int32), pltpu.SemaphoreType.DMA],
        after=[far_n],
    )
    near_blocks, fine_iterate = near_blocks_call(coarse_coupling, iterate, held, last_row, cells)
    far_n = far(far_n)
    even_h, odd_h = even(even_s), odd(odd_s)

    state = [padded(BLOCK_X), field(coarse_cells), padded(COARSE_X)]
    change, coarse_side, coarse_grid, far_m = run(
        "left_middle",
        functools.partial(left_middle_kernel, MIDDLE),
        state + [field(middle)],
        [blocks, side, own_blocks, far_m, change],
        [(4, 0)],
        after=[even_h, odd_h, near_blocks],
        cost=LONG,
    )
    far_m = far(far_m)
    (change,) = run(
        "left_halo", left_halo_kernel, [padded(BLOCK_X)], [near_h, even_h, odd_h, change], [(3, 0)]
    )
    coarse_side, coarse_grid, near_s = run(
        "left_inner",
        left_inner_kernel,
        state[1:] + [field(len(INSIDE))],
        [blocks, side, own_blocks, change, coarse_side, coarse_grid],
        [(4, 0), (5, 1)],
    )
    near_h = near(near_s)
    change, coarse_side, coarse_grid, far_n, even_s, odd_s = run(
        "left_ends",
        functools.partial(left_ends_kernel, ENDS),
        state + [field(ends), field(COARSE_X), field(COARSE_X)],
        [blocks, side, own_blocks, far_n, change, coarse_side, coarse_grid],
        [(4, 0), (5, 1), (6, 2)],
        cost=LONG,
    )
    far_n = far(far_n)
    even_h, odd_h = even(even_s), odd(odd_s)
    coarse_grid, corners, beside = run(
        "pack_first",
        pack_kernel,
        [padded(COARSE_X), field(2), field(len(BORDER))],
        [even_h, odd_h, coarse_grid],
        [(2, 0)],
    )
    corners, beside = lax.ppermute(corners, BOTH, corner_pairs), near(beside)

    state = [padded(COARSE_X), field(coarse_cells), padded(COARSE_X), field(coarse_cells)]
    inner = MIDDLE[1:-1]
    outer = tuple(q for q in range(BLOCK_Y) if q not in inner)
    coarse_grid, coarse_side, coarse_change, iterate, far_m = run(
        "coarse_middle",
        functools.partial(coarse_middle_kernel, MIDDLE, inner),
        state + [field(len(inner))],
        [places, near_blocks, own_blocks, far_m, coarse_grid, coarse_side],
        [(4, 0), (5, 1)],
        smem=(0,),
        cost=LONG,
    )
    far_m = far(far_m)
    (coarse_grid,) = run(
        "coarse_halo", coarse_halo_kernel, [padded(COARSE_X)], [near_h, beside, coarse_grid], [(2, 0)]
    )
    coarse_side, coarse_change, iterate, near_s = run(
        "coarse_inner",
        coarse_inner_kernel,
        state[1:] + [field(len(INSIDE))],
        [places, near_blocks, own_blocks, coarse_grid, coarse_side, coarse_change, iterate],
        [(4, 0), (5, 1), (6, 2)],
        smem=(0,),
    )
    near_h = near(near_s)
    low, high = (tuple(q for q in outer if (q < inner[0]) == first) for first in (True, False))
    coarse_grid, coarse_side, coarse_change, iterate, far_low, far_high, even_s, odd_s = run(
        "coarse_ends",
        functools.partial(coarse_ends_kernel, ENDS, outer),
        state + [field(len(low)), field(len(high)), field(COARSE_X), field(COARSE_X)],
        [places, near_blocks, own_blocks, far_n, corners, coarse_grid, coarse_side, coarse_change, iterate],
        [(5, 0), (6, 1), (7, 2), (8, 3)],
        smem=(0,),
        cost=LONG,
    )
    far_low, far_high = far(far_low), far(far_high)
    even_h, odd_h = even(even_s), odd(odd_s)
    state = [padded(COARSE_X), field(coarse_cells // 2)]
    half = BLOCK_Y // 2
    core = tuple(q // 2 for q in inner[1:-1:2])
    coarse_change, below, coarse_iterate = run(
        "last_inner",
        functools.partial(last_inner_kernel, tuple(range(1, half - 1))),
        state + [field(coarse_cells)],
        [places, near_blocks, own_blocks, coarse_side, near_h, iterate, coarse_change],
        [(6, 0)],
        smem=(0,),
        hbm_outs=(2,),
        scratch=[pltpu.SemaphoreType.DMA],
    )
    coarse_change, corners, beside = run(
        "pack_second",
        pack_kernel,
        [padded(COARSE_X), field(2), field(len(BORDER))],
        [even_h, odd_h, coarse_change],
        [(2, 0)],
    )
    corners, beside = lax.ppermute(corners, BOTH, corner_pairs), near(beside)

    coarse_change, below = run(
        "last_middle",
        functools.partial(last_middle_kernel, inner, core),
        state,
        [places, near_blocks, own_blocks, coarse_side, far_m, coarse_change, below],
        [(5, 0), (6, 1)],
        smem=(0,),
        cost=LONG,
    )
    coarse_change, below = run(
        "last_sides",
        functools.partial(last_sides_kernel, (0, half - 1)),
        state,
        [places, near_blocks, own_blocks, coarse_side, beside, coarse_change, below],
        [(5, 0), (6, 1)],
        smem=(0,),
    )
    coarse_change, below = run(
        "last_low",
        functools.partial(last_low_kernel, low, tuple(range(1, core[0]))),
        state,
        [places, near_blocks, own_blocks, coarse_side, far_low, coarse_change, below],
        [(5, 0), (6, 1)],
        smem=(0,),
    )
    coarse_change, next_side = run(
        "last_high",
        functools.partial(last_high_kernel, high, tuple(range(core[-1] + 1, half))),
        state,
        [places, near_blocks, own_blocks, coarse_side, coarse_change, below, corners, far_high],
        [(4, 0)],
        smem=(0,),
        hbm_outs=(1,),
        scratch=[pltpu.VMEM(state[1][0], F32), pltpu.SemaphoreType.DMA((COARSE_X + 2,))],
        room=3,
    )
    return (fine_iterate, coarse_iterate, next_side)


def solution(mesh):
    placed = (
        P(BOTH, None, None),
        P(BOTH, None, None, None),
        P(BOTH, None, None),
        P(BOTH, None, None),
        P(BOTH, None, None, None),
        P(BOTH, None, None),
        P(BOTH, None, None),
        P(BOTH, None),
    )
    return jax.shard_map(
        on_device,
        mesh=mesh,
        in_specs=placed,
        out_specs=(P(BOTH, None, None), P(BOTH, None, None), P(BOTH, None, None)),
        check_vma=False,
    )
```

```python
import functools

import jax
import jax.numpy as jnp
from jax import lax
from jax.experimental import pallas as pl
from jax.experimental.pallas import tpu as pltpu
from jax.sharding import PartitionSpec as P

BLOCK_X = 4
BLOCK_Y = 32

WIDE = BLOCK_Y + 2
COARSE_X = BLOCK_X // 2
EDGE = BLOCK_Y // 4
MIDDLE = tuple(range(EDGE, BLOCK_Y - EDGE))
ENDS = tuple(q for q in range(BLOCK_Y) if q not in MIDDLE)
SIDES = (0, BLOCK_Y - 1)
BESIDE = (-1, BLOCK_Y)
BORDER = (-1, 0, BLOCK_Y - 1, BLOCK_Y)
INSIDE = tuple(range(1, BLOCK_Y - 1))

F32 = jnp.float32
BF16 = jnp.bfloat16
BOTH = ("gx", "gy")


def split(x):
    high = x.astype(BF16)
    low = (x - high.astype(F32)).astype(BF16)
    return jnp.concatenate([high, low], axis=1)


def fold(x):
    half = x.shape[1] // 2
    return x[:, :half].astype(F32) + x[:, half:].astype(F32)


def dot(*pairs):
    parts = [jnp.dot(a, b, preferred_element_type=F32) for a, b in pairs]
    return fold(functools.reduce(jnp.add, parts))


def row_parity():
    return lax.rem(lax.axis_index("gx"), 2)


def col_parity():
    return lax.rem(lax.axis_index("gy"), 2)


def place(rho, rows):
    parity = row_parity()
    return rho + parity * (rows - 1 - 2 * rho)


def spot(rho, q):
    return (rho + 1) * WIDE + q + 1


def swap_far(rows, cols, hop):
    pairs = []
    for a in range(rows):
        for b in range(cols):
            partner = a - 1 if a % 2 == 0 else a + 1
            if 0 <= partner < rows:
                pairs.append((a * cols + b, partner * cols + b))
            elif hop:
                pairs.append((a * cols + b, a * cols + (b ^ hop)))
    return pairs


def swap_near(rows, cols):
    return [(a * cols + b, (a ^ 1) * cols + b) for a in range(rows) for b in range(cols)]


def swap_even(rows, cols):
    return [(a * cols + b, a * cols + (b ^ 1)) for a in range(rows) for b in range(cols)]


def swap_odd(rows, cols):
    pairs = []
    for a in range(rows):
        for b in range(cols):
            partner = b - 1 if b % 2 == 0 else b + 1
            if 0 <= partner < cols:
                pairs.append((a * cols + b, a * cols + partner))
            else:
                pairs.append((a * cols + b, (a ^ 1) * cols + b))
    return pairs


def far_is_inside():
    gx = lax.axis_index("gx")
    return jnp.where(row_parity() == 0, gx > 0, gx < lax.axis_size("gx") - 1)


def odd_is_inside():
    gy = lax.axis_index("gy")
    return jnp.where(col_parity() == 0, gy > 0, gy < lax.axis_size("gy") - 1)


def write_sides(grid, even_halo, odd_halo, rows):
    parity = col_parity()
    even_col = jnp.where(parity == 0, BLOCK_Y, -1)
    odd_col = BLOCK_Y - 1 - even_col
    inside = odd_is_inside()
    for rho in range(rows):
        grid[spot(rho, even_col)] = split(even_halo[rho])
        grid[spot(rho, odd_col)] = split(jnp.where(inside, odd_halo[rho], 0.0))


def read_sides(grid, even_send, odd_send, rows):
    parity = col_parity()
    even_col = jnp.where(parity == 0, BLOCK_Y - 1, 0)
    odd_col = BLOCK_Y - 1 - even_col
    for rho in range(rows):
        even_send[rho] = fold(grid[spot(rho, even_col)])
        odd_send[rho] = fold(grid[spot(rho, odd_col)])


def write_row(grid, halo, rho, cols, inside=None):
    for n, q in enumerate(cols):
        value = halo[n]
        if inside is not None:
            value = jnp.where(inside, value, 0.0)
        grid[spot(rho, q)] = split(value)


def read_row(grid, send, rho, cols):
    for n, q in enumerate(cols):
        send[n] = fold(grid[spot(rho, q)])


def over_rows(first, last, body):
    def step(rho, carry):
        body(rho)
        return carry

    lax.fori_loop(first, last, step, 0)


def with_zeros(own, after):
    none = jnp.zeros(own.shape, BF16)
    return jnp.concatenate([own, none] if after else [none, own], axis=0)


def smoothed(blocks, cell, side):
    species = side.shape[0]
    return dot((blocks[cell, :, -2 * species :], with_zeros(split(side), False)))


def fine_cell(rho, q):
    return place(rho, BLOCK_X) * BLOCK_Y + q


def fine_apply(rho, q, blocks, grid):
    cell = fine_cell(rho, q)
    species = blocks.shape[1]
    here = spot(rho, q)
    step = WIDE * (1 - 2 * row_parity())
    near = jnp.concatenate([grid[here - step], grid[here + step], grid[here - 1], grid[here + 1]], axis=0)
    return dot(
        (blocks[cell, :, : 4 * species], near), (blocks[cell, :, 4 * species :], with_zeros(grid[here], True))
    )


def fine_second(rho, cols, blocks, grid, side, change, iterate, first, far=None):
    fine_cells([(rho, q, first + q) for q in cols], blocks, grid, side, change, iterate, far)


def fine_cells(cells, blocks, grid, side, change, iterate, far=None):
    for rho, q, _ in cells:
        cell = fine_cell(rho, q)
        side[cell] = side[cell] - fine_apply(rho, q, blocks, grid)
    for m, (rho, q, n) in enumerate(cells):
        cell = fine_cell(rho, q)
        here = spot(rho, q)
        step = smoothed(blocks, cell, side[cell])
        change[here] = split(step)
        iterate[n] = fold(grid[here]) + step
        if far is not None:
            far[m] = step


def fine_left(rho, q, blocks, side, change):
    return side[fine_cell(rho, q)] - fine_apply(rho, q, blocks, change)


def start_kernel(right, inverse, blocks, grid, side, far_m, far_n, inverse_here, sems):
    species = inverse.shape[0]
    part = species // 2
    loads = [
        pltpu.make_async_copy(inverse.at[pl.ds(n * part, part)], inverse_here.at[pl.ds(n * part, part)], sems.at[n])
        for n in range(2)
    ]
    for rho in range(BLOCK_X):
        row = pl.ds(fine_cell(rho, 0), BLOCK_Y)
        loads.append(pltpu.make_async_copy(right.at[row], side.at[row], sems.at[2 + rho]))
    for load in loads:
        load.start()
    for n in range(2):
        loads[n].wait()
        some = inverse_here[n * part : (n + 1) * part]
        both = jnp.concatenate([jnp.zeros(some.shape, BF16), some], axis=1)
        blocks[:, n * part : (n + 1) * part, 4 * species :] = jnp.transpose(both, (2, 0, 1))
    loads[2].wait()
    for cols, send in ((MIDDLE, far_m), (ENDS, far_n)):
        for n, q in enumerate(cols):
            cell = fine_cell(0, q)
            first = smoothed(blocks, cell, side[cell])
            grid[spot(0, q)] = split(first)
            send[n] = first
    for load in loads[3:]:
        load.wait()


def first_kernel(side, blocks, grid_in, grid, near, even, odd):
    def row(rho, near=None):
        for q in range(BLOCK_Y):
            cell = fine_cell(rho, q)
            first = smoothed(blocks, cell, side[cell])
            grid[spot(rho, q)] = split(first)
            if near is not None:
                near[q] = first

    over_rows(1, BLOCK_X - 1, row)
    row(BLOCK_X - 1, near)
    read_sides(grid, even, odd, BLOCK_X)


def fine_blocks_kernel(coupling, diagonal, inverse, blocks_in, blocks):
    species = coupling.shape[0]
    part = species // 2
    for first in range(0, species, part):
        rows = slice(first, first + part)
        blocks[:, rows, : 4 * species] = jnp.transpose(coupling[rows], (2, 0, 1))
        both = jnp.concatenate([diagonal[rows], inverse[rows]], axis=1)
        blocks[:, rows, 4 * species :] = jnp.transpose(both, (2, 0, 1))


def fine_inner_kernel(blocks, grid, side_in, side, change, held):
    for rho in range(1, BLOCK_X - 1):
        fine_second(rho, INSIDE, blocks, grid, side, change, held, (rho - 1) * BLOCK_Y)


def fine_middle_kernel(cols, blocks, far_h, grid_in, side_in, change_in, grid, side, change, iterate, far):
    write_row(grid, far_h, -1, cols, far_is_inside())
    fine_second(0, cols, blocks, grid, side, change, iterate, 0, far)


def fine_last_kernel(
    blocks, near_h, even_h, odd_h, grid_in, side_in, change_in, grid, side, change, last, near
):
    write_row(grid, near_h, BLOCK_X, range(BLOCK_Y))
    write_sides(grid, even_h, odd_h, BLOCK_X)
    fine_second(BLOCK_X - 1, range(BLOCK_Y), blocks, grid, side, change, last, 0, near)


def fine_ends_kernel(
    cols,
    blocks,
    far_h,
    grid_in,
    side_in,
    change_in,
    iterate_in,
    held_in,
    grid,
    side,
    change,
    iterate,
    held,
    far,
    even,
    odd,
):
    write_row(grid, far_h, -1, cols, far_is_inside())
    fine_second(0, cols, blocks, grid, side, change, iterate, 0, far)
    others = [(rho, q, (rho - 1) * BLOCK_Y + q) for rho in range(1, BLOCK_X - 1) for q in SIDES]
    fine_cells(others, blocks, grid, side, change, held)
    read_sides(change, even, odd, BLOCK_X)


def left_pair(rho, cols, blocks, side, change, coarse_side, own_blocks, coarse_grid, far=None, shift=0):
    for q in cols:
        upper = fine_left(2 * rho, q, blocks, side, change)
        coarse_side[rho * BLOCK_Y + q] = upper + fine_left(2 * rho + 1, q, blocks, side, change)
    for n, q in enumerate(cols):
        cell = place(rho, COARSE_X) * BLOCK_Y + q
        first = smoothed(own_blocks, cell, coarse_side[rho * BLOCK_Y + q])
        coarse_grid[spot(rho, q)] = split(first)
        if far is not None:
            far[n + shift] = first


def left_middle_kernel(cols, blocks, side, own_blocks, far_h, change_in, change, coarse_side, coarse_grid, far):
    write_row(change, far_h, -1, cols, far_is_inside())
    left_pair(0, cols, blocks, side, change, coarse_side, own_blocks, coarse_grid, far)


def left_halo_kernel(near_h, even_h, odd_h, change_in, change):
    write_row(change, near_h, BLOCK_X, range(BLOCK_Y))
    write_sides(change, even_h, odd_h, BLOCK_X)


def left_ends_kernel(
    cols,
    blocks,
    side,
    own_blocks,
    far_h,
    change_in,
    coarse_in,
    grid_in,
    change,
    coarse_side,
    coarse_grid,
    far,
    even,
    odd,
):
    write_row(change, far_h, -1, cols, far_is_inside())
    left_pair(0, cols, blocks, side, change, coarse_side, own_blocks, coarse_grid, far)
    for rho in range(1, COARSE_X):
        left_pair(rho, SIDES, blocks, side, change, coarse_side, own_blocks, coarse_grid)
    read_sides(coarse_grid, even, odd, COARSE_X)


def left_inner_kernel(blocks, side, own_blocks, change, coarse_in, grid_in, coarse_side, coarse_grid, near):
    for rho in range(1, COARSE_X):
        last = near if rho == COARSE_X - 1 else None
        left_pair(rho, INSIDE, blocks, side, change, coarse_side, own_blocks, coarse_grid, last)


def near_blocks_kernel(coupling, first_row, held, last_row, blocks, out, sems):
    species = coupling.shape[1]
    step, count = pl.program_id(0), coupling.shape[0]
    copies = []
    for rho in range(BLOCK_X):
        source = first_row if rho == 0 else last_row
        if 0 < rho < BLOCK_X - 1:
            source = held.at[pl.ds((rho - 1) * BLOCK_Y, BLOCK_Y)]
        target = out.at[pl.ds(fine_cell(rho, 0), BLOCK_Y)]
        copies.append(pltpu.make_async_copy(source, target, sems.at[rho]))

    @pl.when(step == 0)
    def _():
        for copy in copies:
            copy.start()

    for n in range(count):
        blocks[step * count + n] = coupling[n].reshape(species, 8 * species)

    @pl.when(step == pl.num_programs(0) - 1)
    def _():
        for copy in copies:
            copy.wait()


def coarse_apply(rho, q, places, blocks, own_blocks, grid):
    cell = place(rho, COARSE_X) * BLOCK_Y + q
    near = jnp.concatenate([grid[places[k, cell]] for k in range(8)], axis=0)
    return dot((blocks[cell], near), (own_blocks[cell], with_zeros(grid[spot(rho, q)], True)))


def coarse_second(rho, cols, places, blocks, own_blocks, grid, side, change, iterate, far=None, shift=0):
    for q in cols:
        here = rho * BLOCK_Y + q
        side[here] = side[here] - coarse_apply(rho, q, places, blocks, own_blocks, grid)
    for m, q in enumerate(cols):
        here = spot(rho, q)
        cell = place(rho, COARSE_X) * BLOCK_Y + q
        step = smoothed(own_blocks, cell, side[rho * BLOCK_Y + q])
        change[here] = split(step)
        iterate[cell] = fold(grid[here]) + step
        if far is not None:
            far[m + shift] = step


def pack_kernel(even_h, odd_h, grid_in, grid, far, near):
    write_sides(grid, even_h, odd_h, COARSE_X)
    read_row(grid, far, 0, BESIDE)
    read_row(grid, near, COARSE_X - 1, BORDER)


def coarse_inner_kernel(places, blocks, own_blocks, grid, side_in, change_in, iterate_in, side, change, iterate, near):
    for rho in range(1, COARSE_X):
        last = near if rho == COARSE_X - 1 else None
        coarse_second(rho, INSIDE, places, blocks, own_blocks, grid, side, change, iterate, last)


def coarse_halo_kernel(near_h, beside_h, grid_in, grid):
    write_row(grid, near_h, COARSE_X, INSIDE)
    write_row(grid, beside_h, COARSE_X, BORDER)


def coarse_middle_kernel(
    came, cols, places, blocks, own_blocks, far_h, grid_in, side_in, grid, side, change, iterate, far
):
    write_row(grid, far_h, -1, came)
    coarse_second(0, cols, places, blocks, own_blocks, grid, side, change, iterate, far)


class InTwo:
    def __init__(self, low, high):
        self.low, self.high = low, high

    def __setitem__(self, n, value):
        count = self.low.shape[0]
        if n < count:
            self.low[n] = value
        else:
            self.high[n - count] = value


def coarse_ends_kernel(
    came,
    cols,
    places,
    blocks,
    own_blocks,
    far_h,
    corners_h,
    grid_in,
    side_in,
    change_in,
    iterate_in,
    grid,
    side,
    change,
    iterate,
    low,
    high,
    even,
    odd,
):
    far = InTwo(low, high)
    write_row(grid, far_h, -1, came)
    write_row(grid, corners_h, -1, BESIDE)
    coarse_second(0, cols, places, blocks, own_blocks, grid, side, change, iterate, far)
    for rho in range(1, COARSE_X):
        coarse_second(rho, SIDES, places, blocks, own_blocks, grid, side, change, iterate)
    read_sides(change, even, odd, COARSE_X)


def last_pairs(rho, pairs, places, blocks, own_blocks, side, change, below):
    first = place(rho, COARSE_X) * (BLOCK_Y // 2)
    for pair in pairs:
        q = 2 * pair
        total = side[rho * BLOCK_Y + q] + side[rho * BLOCK_Y + q + 1]
        total = total - coarse_apply(rho, q, places, blocks, own_blocks, change)
        total = total - coarse_apply(rho, q + 1, places, blocks, own_blocks, change)
        below[first + pair] = total


def last_middle_kernel(came, pairs, places, blocks, own_blocks, side, far_h, change_in, below_in, change, below):
    write_row(change, far_h, -1, came)
    last_pairs(0, pairs, places, blocks, own_blocks, side, change, below)


def last_inner_kernel(
    pairs, places, blocks, own_blocks, side, near_h, iterate, change_in, change, below, out, sem
):
    leave = pltpu.make_async_copy(iterate, out, sem)
    leave.start()
    write_row(change, near_h, COARSE_X, INSIDE)
    for rho in range(1, COARSE_X):
        last_pairs(rho, pairs, places, blocks, own_blocks, side, change, below)
    leave.wait()


def last_sides_kernel(todo, places, blocks, own_blocks, side, beside_h, change_in, below_in, change, below):
    write_row(change, beside_h, COARSE_X, BORDER)
    for rho in range(1, COARSE_X):
        last_pairs(rho, todo, places, blocks, own_blocks, side, change, below)


def last_low_kernel(came, todo, places, blocks, own_blocks, side, far_h, change_in, below_in, change, below):
    write_row(change, far_h, -1, came)
    last_pairs(0, todo, places, blocks, own_blocks, side, change, below)


def last_high_kernel(
    came, todo, places, blocks, own_blocks, side, change_in, below, corners_h, far_h, change, out, made, sems
):
    half = BLOCK_Y // 2
    copies = []

    def send(source, rho, first, count):
        some = pl.ds(place(rho, COARSE_X) * half + first, count)
        copies.append(pltpu.make_async_copy(source.at[some], out.at[some], sems.at[len(copies)]))
        copies[-1].start()

    for rho in range(1, COARSE_X):
        send(below, rho, 0, half)
    send(below, 0, 1, todo[0] - 1)
    write_row(change, corners_h, -1, BESIDE)
    write_row(change, far_h, -1, came)
    last_pairs(0, (0,) + todo, places, blocks, own_blocks, side, change, made)
    send(made, 0, 0, 1)
    send(made, 0, todo[0], len(todo))
    for copy in copies:
        copy.wait()


IN_VMEM = pl.BlockSpec(memory_space=pltpu.VMEM)
IN_HBM = pl.BlockSpec(memory_space=pltpu.HBM)
LONG = 10**11


def run(name, kernel, outs, args, aliases=(), smem=(), hbm=(), hbm_outs=(), smem_outs=(), scratch=(), after=(), cost=1, room=2):
    count = len(args)
    args = list(args) + list(after)
    spaces = [pltpu.SMEM if n in smem else pltpu.HBM if n in hbm else pltpu.VMEM for n in range(len(args))]
    out_spaces = [
        pltpu.SMEM if n in smem_outs else pltpu.HBM if n in hbm_outs else pltpu.VMEM for n in range(len(outs))
    ]

    def body(*refs):
        kernel(*refs[:count], *refs[len(args) :])

    called = pl.pallas_call(
        body,
        out_shape=tuple(space(shape, dtype) for space, (shape, dtype) in zip(out_spaces, outs)),
        in_specs=[pl.BlockSpec(memory_space=space) for space in spaces],
        out_specs=tuple(pl.BlockSpec(memory_space=space) for space in out_spaces),
        scratch_shapes=list(scratch),
        input_output_aliases=dict(aliases),
        compiler_params=pltpu.CompilerParams(vmem_limit_bytes=room * 2**20),
        cost_estimate=pl.CostEstimate(flops=cost, bytes_accessed=1, transcendentals=0),
        name=name,
    )
    return called(*(pltpu.with_memory_space_constraint(x, space) for x, space in zip(args, spaces)))


def near_blocks_call(coupling, first_row, held, last_row, count):
    cells, species = coupling.shape[:2]
    part = cells // 4
    here = [pltpu.with_memory_space_constraint(x, pltpu.VMEM) for x in (first_row, held, last_row)]
    return pl.pallas_call(
        near_blocks_kernel,
        grid=(cells // part,),
        out_shape=(
            pltpu.VMEM((cells, species, 8 * species), BF16),
            pltpu.HBM((count,) + first_row.shape[1:], F32),
        ),
        in_specs=[
            pl.BlockSpec((part,) + coupling.shape[1:], lambda n: (n, 0, 0, 0)),
            IN_VMEM,
            IN_VMEM,
            IN_VMEM,
        ],
        out_specs=(IN_VMEM, IN_HBM),
        scratch_shapes=[pltpu.SemaphoreType.DMA((BLOCK_X,))],
        compiler_params=pltpu.CompilerParams(vmem_limit_bytes=7 * 2**20),
        cost_estimate=pl.CostEstimate(flops=1, bytes_accessed=1, transcendentals=0),
        name="near_blocks",
    )(coupling, *here)


def own_blocks_kernel(across, diagonal, inverse, pattern, blocks, places, made, sem):
    number = pattern[...]
    per_block = COARSE_X * BLOCK_Y
    owner = lax.div(number, per_block)
    inside = lax.rem(number, per_block)
    row = lax.div(owner, across) * COARSE_X + lax.div(inside, BLOCK_Y) - lax.axis_index("gx") * COARSE_X
    col = lax.rem(owner, across) * BLOCK_Y + lax.rem(inside, BLOCK_Y) - lax.axis_index("gy") * BLOCK_Y
    rho = jnp.where(row_parity() == 0, row, COARSE_X - 1 - row)
    made[...] = (rho + 1) * WIDE + col + 1
    copy = pltpu.make_async_copy(made, places, sem)
    copy.start()
    for cell in range(diagonal.shape[0]):
        blocks[cell] = jnp.concatenate([diagonal[cell], inverse[cell]], axis=1)
    copy.wait()


def on_device(
    right_side,
    fine_coupling,
    fine_diagonal,
    fine_inverse,
    coarse_coupling,
    coarse_diagonal,
    coarse_inverse,
    coarse_pattern,
):
    cells, species, vectors = right_side.shape
    coarse_cells = coarse_coupling.shape[0]
    rows, cols = lax.axis_size("gx"), lax.axis_size("gy")
    far_pairs, near_pairs = swap_far(rows, cols, 2 if cols % 4 == 0 else 1), swap_near(rows, cols)
    corner_pairs = swap_far(rows, cols, 1)
    even_pairs, odd_pairs = swap_even(rows, cols), swap_odd(rows, cols)

    def far(x):
        return lax.ppermute(x, BOTH, far_pairs)

    def near(x):
        return lax.ppermute(x, BOTH, near_pairs)

    def even(x):
        return lax.ppermute(x, BOTH, even_pairs)

    def odd(x):
        return lax.ppermute(x, BOTH, odd_pairs)

    def field(count):
        return ((count, species, vectors), F32)

    def padded(count):
        return (((count + 2) * WIDE, species, 2 * vectors), BF16)

    fine_blocks = ((cells, species, 6 * species), BF16)
    coupling = jnp.transpose(fine_coupling, (1, 2, 3, 0)).reshape(species, 4 * species, cells)
    diagonal = jnp.transpose(fine_diagonal, (1, 2, 0))
    inverse = jnp.transpose(fine_inverse, (1, 2, 0))
    pattern = coarse_pattern.T
    middle, ends = len(MIDDLE), len(ENDS)

    blocks, grid, side, far_m, far_n = run(
        "start",
        start_kernel,
        [fine_blocks, padded(BLOCK_X), field(cells), field(middle), field(ends)],
        [right_side, inverse],
        hbm=(0, 1),
        scratch=[pltpu.VMEM(inverse.shape, BF16), pltpu.SemaphoreType.DMA((2 + BLOCK_X,))],
        room=6,
    )
    far_m, far_n = lax.ppermute(far_m, BOTH, swap_far(rows, cols, 0)), far(far_n)
    grid, near_s, even_s, odd_s = run(
        "first",
        first_kernel,
        [padded(BLOCK_X), field(BLOCK_Y), field(BLOCK_X), field(BLOCK_X)],
        [side, blocks, grid],
        [(2, 0)],
    )
    near_h, even_h, odd_h = near(near_s), even(even_s), odd(odd_s)
    (blocks,) = run(
        "fine_blocks",
        fine_blocks_kernel,
        [fine_blocks],
        [coupling, diagonal, inverse, blocks],
        [(3, 0)],
        after=[near_s],
        room=6,
    )
    state = [padded(BLOCK_X), field(cells), padded(BLOCK_X)]
    side, change, held = run(
        "fine_inner",
        fine_inner_kernel,
        state[1:] + [field((BLOCK_X - 2) * BLOCK_Y)],
        [blocks, grid, side],
        [(2, 0)],
    )
    grid, side, change, iterate, far_m = run(
        "fine_middle",
        functools.partial(fine_middle_kernel, MIDDLE),
        state + [field(BLOCK_Y), field(middle)],
        [blocks, far_m, grid, side, change],
        [(2, 0), (3, 1), (4, 2)],
        after=[even_h, odd_h],
        cost=LONG,
    )
    far_m = far(far_m)
    grid, side, change, last_row, near_s = run(
        "fine_last",
        fine_last_kernel,
        state + [field(BLOCK_Y), field(BLOCK_Y)],
        [blocks, near_h, even_h, odd_h, grid, side, change],
        [(4, 0), (5, 1), (6, 2)],
    )
    near_h = near(near_s)
    grid, side, change, iterate, held, far_n, even_s, odd_s = run(
        "fine_ends",
        functools.partial(fine_ends_kernel, ENDS),
        state
        + [field(BLOCK_Y), field((BLOCK_X - 2) * BLOCK_Y), field(ends), field(BLOCK_X), field(BLOCK_X)],
        [blocks, far_n, grid, side, change, iterate, held],
        [(2, 0), (3, 1), (4, 2), (5, 3), (6, 4)],
    )
    own_blocks, places = run(
        "own_blocks",
        functools.partial(own_blocks_kernel, cols),
        [((coarse_cells, species, 2 * species), BF16), (pattern.shape, jnp.int32)],
        [coarse_diagonal, coarse_inverse, pattern],
        smem_outs=(1,),
        scratch=[pltpu.VMEM(pattern.shape, jnp.int32), pltpu.SemaphoreType.DMA],
        after=[far_n],
    )
    near_blocks, fine_iterate = near_blocks_call(coarse_coupling, iterate, held, last_row, cells)
    far_n = far(far_n)
    even_h, odd_h = even(even_s), odd(odd_s)

    state = [padded(BLOCK_X), field(coarse_cells), padded(COARSE_X)]
    change, coarse_side, coarse_grid, far_m = run(
        "left_middle",
        functools.partial(left_middle_kernel, MIDDLE),
        state + [field(middle)],
        [blocks, side, own_blocks, far_m, change],
        [(4, 0)],
        after=[even_h, odd_h, near_blocks],
        cost=LONG,
    )
    far_m = far(far_m)
    (change,) = run(
        "left_halo", left_halo_kernel, [padded(BLOCK_X)], [near_h, even_h, odd_h, change], [(3, 0)]
    )
    coarse_side, coarse_grid, near_s = run(
        "left_inner",
        left_inner_kernel,
        state[1:] + [field(len(INSIDE))],
        [blocks, side, own_blocks, change, coarse_side, coarse_grid],
        [(4, 0), (5, 1)],
    )
    near_h = near(near_s)
    change, coarse_side, coarse_grid, far_n, even_s, odd_s = run(
        "left_ends",
        functools.partial(left_ends_kernel, ENDS),
        state + [field(ends), field(COARSE_X), field(COARSE_X)],
        [blocks, side, own_blocks, far_n, change, coarse_side, coarse_grid],
        [(4, 0), (5, 1), (6, 2)],
        cost=LONG,
    )
    far_n = far(far_n)
    even_h, odd_h = even(even_s), odd(odd_s)
    coarse_grid, corners, beside = run(
        "pack_first",
        pack_kernel,
        [padded(COARSE_X), field(2), field(len(BORDER))],
        [even_h, odd_h, coarse_grid],
        [(2, 0)],
    )
    corners, beside = lax.ppermute(corners, BOTH, corner_pairs), near(beside)

    state = [padded(COARSE_X), field(coarse_cells), padded(COARSE_X), field(coarse_cells)]
    inner = MIDDLE[1:-1]
    outer = tuple(q for q in range(BLOCK_Y) if q not in inner)
    coarse_grid, coarse_side, coarse_change, iterate, far_m = run(
        "coarse_middle",
        functools.partial(coarse_middle_kernel, MIDDLE, inner),
        state + [field(len(inner))],
        [places, near_blocks, own_blocks, far_m, coarse_grid, coarse_side],
        [(4, 0), (5, 1)],
        smem=(0,),
        cost=LONG,
    )
    far_m = far(far_m)
    (coarse_grid,) = run(
        "coarse_halo", coarse_halo_kernel, [padded(COARSE_X)], [near_h, beside, coarse_grid], [(2, 0)]
    )
    coarse_side, coarse_change, iterate, near_s = run(
        "coarse_inner",
        coarse_inner_kernel,
        state[1:] + [field(len(INSIDE))],
        [places, near_blocks, own_blocks, coarse_grid, coarse_side, coarse_change, iterate],
        [(4, 0), (5, 1), (6, 2)],
        smem=(0,),
    )
    near_h = near(near_s)
    low, high = (tuple(q for q in outer if (q < inner[0]) == first) for first in (True, False))
    coarse_grid, coarse_side, coarse_change, iterate, far_low, far_high, even_s, odd_s = run(
        "coarse_ends",
        functools.partial(coarse_ends_kernel, ENDS, outer),
        state + [field(len(low)), field(len(high)), field(COARSE_X), field(COARSE_X)],
        [places, near_blocks, own_blocks, far_n, corners, coarse_grid, coarse_side, coarse_change, iterate],
        [(5, 0), (6, 1), (7, 2), (8, 3)],
        smem=(0,),
        cost=LONG,
    )
    far_low, far_high = (lax.ppermute(x, BOTH, corner_pairs) for x in (far_low, far_high))
    even_h, odd_h = even(even_s), odd(odd_s)
    state = [padded(COARSE_X), field(coarse_cells // 2)]
    half = BLOCK_Y // 2
    core = tuple(q // 2 for q in inner[1:-1:2])
    coarse_change, below, coarse_iterate = run(
        "last_inner",
        functools.partial(last_inner_kernel, tuple(range(1, half - 1))),
        state + [field(coarse_cells)],
        [places, near_blocks, own_blocks, coarse_side, near_h, iterate, coarse_change],
        [(6, 0)],
        smem=(0,),
        hbm_outs=(2,),
        scratch=[pltpu.SemaphoreType.DMA],
    )
    coarse_change, corners, beside = run(
        "pack_second",
        pack_kernel,
        [padded(COARSE_X), field(2), field(len(BORDER))],
        [even_h, odd_h, coarse_change],
        [(2, 0)],
    )
    corners, beside = lax.ppermute(corners, BOTH, corner_pairs), near(beside)

    coarse_change, below = run(
        "last_middle",
        functools.partial(last_middle_kernel, inner, core),
        state,
        [places, near_blocks, own_blocks, coarse_side, far_m, coarse_change, below],
        [(5, 0), (6, 1)],
        smem=(0,),
        cost=LONG,
    )
    coarse_change, below = run(
        "last_sides",
        functools.partial(last_sides_kernel, (0, half - 1)),
        state,
        [places, near_blocks, own_blocks, coarse_side, beside, coarse_change, below],
        [(5, 0), (6, 1)],
        smem=(0,),
    )
    coarse_change, below = run(
        "last_low",
        functools.partial(last_low_kernel, low, tuple(range(1, core[0]))),
        state,
        [places, near_blocks, own_blocks, coarse_side, far_low, coarse_change, below],
        [(5, 0), (6, 1)],
        smem=(0,),
    )
    coarse_change, next_side = run(
        "last_high",
        functools.partial(last_high_kernel, high, tuple(range(core[-1] + 1, half))),
        state,
        [places, near_blocks, own_blocks, coarse_side, coarse_change, below, corners, far_high],
        [(4, 0)],
        smem=(0,),
        hbm_outs=(1,),
        scratch=[pltpu.VMEM(state[1][0], F32), pltpu.SemaphoreType.DMA((COARSE_X + 2,))],
        room=3,
    )
    return (fine_iterate, coarse_iterate, next_side)


def solution(mesh):
    placed = (
        P(BOTH, None, None),
        P(BOTH, None, None, None),
        P(BOTH, None, None),
        P(BOTH, None, None),
        P(BOTH, None, None, None),
        P(BOTH, None, None),
        P(BOTH, None, None),
        P(BOTH, None),
    )
    return jax.shard_map(
        on_device,
        mesh=mesh,
        in_specs=placed,
        out_specs=(P(BOTH, None, None), P(BOTH, None, None), P(BOTH, None, None)),
        check_vma=False,
    )
```
